256 devices in a mesh: row: 8 (over z), col: 32 (over y, x, core).
Axes of the slice: x: 4, y: 4, z: 8, core: 2. Of those that a mesh axis runs over, the one named last changes fastest.
Arguments:
- resident: float32 [12288, 12288], P('row', 'col'), may hold values from -6 to 6
- factor_one: float32 [12288, 512], P(('row', 'col')), may hold values from -0.0546875 to 0.0546875
- pattern_one: int32 [768], P(('row', 'col')), may hold values 0 or 1
- factor_two: float32 [12288, 512], P(('row', 'col')), may hold values from -0.0546875 to 0.0546875
- pattern_two: int32 [768], P(('row', 'col')), may hold values 0 or 1
- coupling: float32 [512, 512], replicated, may hold values from -0.25 to 0.25
- diagonal_one: float32 [512, 512], replicated, may hold values from -6 to 6
- diagonal_two: float32 [512, 512], replicated, may hold values from -6 to 6
Outputs:
- inverse_one: float32 [12288, 512], P(('row', 'col'))
- block_one: float32 [512, 512], replicated
- inverse_two: float32 [12288, 512], P(('row', 'col'))
- coupled: float32 [512, 512], replicated
- block_two: float32 [512, 512], replicated
The draws below stay inside these ranges and needn't reach their ends.
Inputs may be any that keep to these rules, and one draw needn't show every extreme that they name: `pattern_one`: 1 keeps a block of 16 factor rows, 0 marks it structurally zero. `pattern_two`: 1 keeps a block of 16 factor rows, 0 marks it structurally zero.
All inputs are finite; a program needn't handle non-finite values.
Results may differ from the reference program's by a relative error of at most 0.00007.
Values sent between devices are 32-bit elements; how exact they have to be, the bound alone decides.
A program may use at most 64 MiB of HBM per device.

```python
import jax
import jax.numpy as jnp
from jax import lax

W = 512
ORDER = 12288
NBLK = 768


def set_ends(entries, own_key, low, largest):
    index_at = [jax.random.randint(jax.random.fold_in(own_key, axis), (), 0, length) for axis, length in enumerate(entries.shape)]
    widest = entries.shape.index(max(entries.shape))
    beside = index_at[:widest] + [(index_at[widest] + 1) % entries.shape[widest]] + index_at[widest + 1:]
    return entries.at[tuple(index_at)].set(low).at[tuple(beside)].set(largest)


def shard_levels(key, extent, split, least, top_value):
    level = 1.0
    for axis_at, blocks in split:
        steps = jax.random.uniform(jax.random.fold_in(jax.random.fold_in(key, 6), axis_at), (blocks,), jnp.float32, least / len(split), top_value / len(split))
        level = level * jnp.repeat(jnp.exp(steps), extent[axis_at] // blocks).reshape((-1,) + (1,) * (len(extent) - 1 - axis_at))
    return level


def scatter_about(stream_key, dims, spread, limit, shards=(), dtype=jnp.bfloat16):
    entries = jax.random.normal(stream_key, dims, jnp.float32) * spread
    if len(shards) > 0:
        entries = shard_levels(stream_key, dims, shards, -0.22, 0.18) * entries
    return jnp.clip(entries, min=-limit, max=limit).astype(dtype)


def setup_inputs(seed: int = 0) -> dict:
    splits = jax.random.split(jax.random.key(seed), 9)
    return {
        "resident": scatter_about(splits[0], (ORDER, ORDER), 1.0, 6.0, ((0, 8), (1, 32)), jnp.float32),
        "factor_one": scatter_about(splits[1], (ORDER, W), ORDER ** -0.5, 0.0546875, ((0, 256),), jnp.float32),
        "pattern_one": set_ends((jax.random.randint(splits[2], (NBLK,), 0, 4) < 3).astype(jnp.int32), jax.random.fold_in(splits[2], 1), 0, 1),
        "factor_two": scatter_about(splits[3], (ORDER, W), ORDER ** -0.5, 0.0546875, ((0, 256),), jnp.float32),
        "pattern_two": set_ends((jax.random.randint(splits[4], (NBLK,), 0, 4) < 3).astype(jnp.int32), jax.random.fold_in(splits[4], 1), 0, 1),
        "coupling": scatter_about(splits[5], (W, W), W ** -0.5, 0.25, (), jnp.float32),
        "diagonal_one": scatter_about(splits[6], (W, W), 1.0, 6.0, (), jnp.float32),
        "diagonal_two": scatter_about(splits[7], (W, W), 1.0, 6.0, (), jnp.float32),
    }


def masked(factor, pattern):
    block_count = pattern.shape[0]
    row_count, col_width = factor.shape
    shaped = factor.reshape(block_count, row_count // block_count, col_width)
    return (shaped * pattern.astype(jnp.float32)[:, None, None]).reshape(row_count, col_width)


def reference(resident, factor_one, pattern_one, factor_two, pattern_two, coupling, diagonal_one, diagonal_two):
    high = lax.Precision.HIGHEST
    first = masked(factor_one, pattern_one)
    second = masked(factor_two, pattern_two)
    inverse_one = -jnp.dot(resident, first, precision=high, preferred_element_type=jnp.float32)
    block_one = diagonal_one - jnp.einsum("ka,kb->ab", first, inverse_one, precision=high)
    coupled = -(jnp.einsum("ka,kb->ab", inverse_one, second, precision=high) + jnp.dot(block_one, coupling, precision=high))
    inverse_two = -(jnp.dot(resident, second, precision=high, preferred_element_type=jnp.float32) + jnp.dot(inverse_one, coupling, precision=high))
    block_two = diagonal_two - jnp.einsum("ka,kb->ab", second, inverse_two, precision=high) - jnp.einsum("ka,kb->ab", coupling, coupled, precision=high)
    return (inverse_one, block_one, inverse_two, coupled, block_two)
```

```python
import jax
import jax.numpy as jnp
from jax import lax
from jax.experimental import pallas as pl
from jax.experimental.pallas import tpu as pltpu
from jax.sharding import PartitionSpec as P

W = 512
MESH = pl.DeviceIdType.MESH
BF = jnp.bfloat16
F32 = jnp.float32
TURN, SHIFT = 3, 1


def halves(value):
    high = value.astype(BF)
    return high, (value - high.astype(F32)).astype(BF)


def dot3(left, right):
    (lh, ll), (rh, rl) = left, right
    total = jnp.dot(lh, rh, preferred_element_type=F32)
    total += jnp.dot(lh, rl, preferred_element_type=F32)
    return total + jnp.dot(ll, rh, preferred_element_type=F32)


class Mail:
    def __init__(self, send, recv):
        self.send, self.recv, self.count, self.sent = send, recv, 0, []

    def slots(self, n):
        first = self.count
        self.count += n
        return list(range(first, first + n))

    def desc(self, slot, src, dst, dev):
        return pltpu.make_async_remote_copy(
            src, dst, self.send.at[slot], self.recv.at[slot], device_id=dev, device_id_type=MESH
        )

    def post(self, slot, src, dst, dev):
        copy = self.desc(slot, src, dst, dev)
        copy.start()
        self.sent.append(copy)

    def take(self, slot, dst, dev):
        self.desc(slot, dst, dst, dev).wait_recv()


N_MAIL = 200
N_LOCAL = 40


def kernel(
    res, fac1, pat1, fac2, pat2, coup, diag1, diag2,
    inv1_o, blk1_o, inv2_o, cpl_o, blk2_o,
    own, rx, rh, rl, g, gh, gl, p, ra, rb, s, sa, sb, t, ib, tx, fy, ft, ftb, ftx,
    cb, cx, cz, cf, kk_v, d1_v, d2_v, o1, o2, ob1, ob2, oc,
    send, recv, local,
):
    z = lax.axis_index("row")
    col = lax.axis_index("col")
    k = col % 2
    x = (col // 2) % 4
    y = col // 8
    other = 1 - k

    def at(xx, yy, zz, kk):
        return (zz, (yy * 4 + xx) * 2 + kk)

    partner = at(x, y, z, other)

    def zdev(d):
        return at(x, y, (z + d + 8) % 8, k)

    def xdev(d):
        return at((x + d + 4) % 4, y, z, k)

    def ydev(d):
        return at(x, (y + d + 4) % 4, z, k)

    u = x + k * (y - x)
    v = y + k * (x - y)

    def udev(d):
        return at((x + (1 - k) * d + 4) % 4, (y + k * d + 4) % 4, z, k)

    def vdev(d):
        return at((x + k * d + 4) % 4, (y + (1 - k) * d + 4) % 4, z, k)

    mine = (y % 2) * 4 + x
    goal = 2 * z + y // 2
    target = at(goal % 4, goal // 4, (mine + TURN * z + SHIFT) % 8, k)
    q = 4 * y + x
    z0 = q // 2

    def chunk(zz):
        return (zz + 64 - TURN * z0 - SHIFT) % 8

    first_i = chunk(z)
    source = at(first_i % 4, 2 * (q % 2) + first_i // 4, z0, k)

    mail = Mail(send, recv)
    used = [0]

    def here(src, dst):
        copy = pltpu.make_async_copy(src, dst, local.at[used[0]])
        used[0] += 1
        copy.start()
        return copy

    load_f = [here(fac1, own.at[0]), here(fac2, own.at[1])]
    load_r = [here(res.at[:, a, k], rx.at[k, a]) for a in range(4)]
    load_k = here(coup, kk_v)
    load_d1 = here(diag1, d1_v)
    load_d2 = here(diag2, d2_v)

    barrier = pltpu.get_barrier_semaphore()
    friends = [partner] + [zdev(d) for d in range(1, 8)] + [xdev(d) for d in range(1, 4)] + [ydev(d) for d in range(1, 4)]
    for dev in friends + [source]:
        pl.semaphore_signal(barrier, inc=1, device_id=dev, device_id_type=MESH)

    for j, pat in ((0, pat1), (1, pat2)):
        load_f[j].wait()
        for b in range(3):
            own[j, 16 * b : 16 * b + 16] = own[j, 16 * b : 16 * b + 16] * pat[b].astype(F32)
    pl.semaphore_wait(barrier, len(friends) + 1)

    slot_perm = mail.slots(2)
    slot_r = mail.slots(4)
    slot_fx = mail.slots(1)[0]
    mail.post(slot_perm[0], own.at[0], g.at[0, 2 * mine + k], target)
    for a in range(4):
        mail.post(slot_r[a], res.at[:, a, other], rx.at[k, a], partner)
    mail.post(slot_perm[1], own.at[1], g.at[1, 2 * mine + k], target)
    fy[y, k] = own[k]
    mail.post(slot_fx, own.at[other], fy.at[y, k], partner)

    slot_up = [mail.slots(4), mail.slots(4)]
    slot_dn = [mail.slots(4), mail.slots(4)]
    slot_fwd = [mail.slots(8), mail.slots(8)]

    def split(j, m):
        gh[j, m], gl[j, m] = halves(g[j, m])

    def forward(j, f, zz):
        m = 2 * chunk(zz) + k
        mail.post(slot_fwd[j][f], g.at[j, m], g.at[j, m], partner)
        split(j, m)

    def arrived(j, f, zz):
        m = 2 * chunk(zz) + other
        mail.take(slot_fwd[j][f], g.at[j, m], partner)
        split(j, m)

    order = [0, -1, 1, -2, 2, -3, 3, 4]

    def ring(j, step):
        m_up = 2 * chunk(z + 8 - step) + k
        m_dn = 2 * chunk(z + step) + k
        if step == 0:
            mail.take(slot_perm[j], g.at[j, m_up], target)
            mail.post(slot_up[j][0], g.at[j, m_up], g.at[j, m_up], zdev(1))
            mail.post(slot_dn[j][0], g.at[j, m_up], g.at[j, m_up], zdev(-1))
            forward(j, 0, z)
            return
        lo = g.at[j, m_up]
        hi = g.at[j, m_dn]
        if step == 4:
            mail.take(slot_up[j][3], lo.at[pl.ds(0, 24)], zdev(1))
            mail.take(slot_dn[j][3], hi.at[pl.ds(24, 24)], zdev(-1))
            forward(j, 7, z + 4)
            return
        if step == 3:
            lo, hi = lo, hi
        mail.take(slot_up[j][step - 1], g.at[j, m_up], zdev(1))
        if step == 3:
            mail.post(slot_up[j][3], lo.at[pl.ds(0, 24)], lo.at[pl.ds(0, 24)], zdev(1))
        else:
            mail.post(slot_up[j][step], lo, lo, zdev(1))
        mail.take(slot_dn[j][step - 1], g.at[j, m_dn], zdev(-1))
        if step == 3:
            mail.post(slot_dn[j][3], hi.at[pl.ds(24, 24)], hi.at[pl.ds(24, 24)], zdev(-1))
        else:
            mail.post(slot_dn[j][step], hi, hi, zdev(-1))
        forward(j, 2 * step - 1, z + 8 - step)
        forward(j, 2 * step, z + step)

    def collect(j, step):
        if step in (0, 4):
            f = 0 if step == 0 else 7
            arrived(j, f, z + order[f] + 8)
        else:
            arrived(j, 2 * step - 1, z + 8 - step)
            arrived(j, 2 * step, z + step)

    def split_r(cc, dyn):
        for a in range(4):
            hi, lo = halves(rx[dyn, a].reshape(192, 384))
            rh[a, :, pl.ds(pl.multiple_of(dyn * 384, 128), 384)] = hi
            rl[a, :, pl.ds(pl.multiple_of(dyn * 384, 128), 384)] = lo

    def product(j, a0, a1):
        def one(a, carry):
            gj = (gh[j].reshape(768, W), gl[j].reshape(768, W))
            got = dot3((rh[a], rl[a]), gj)
            for b in range(4):
                p[j, a + k * (b - a), b + k * (a - b)] = got[:, 128 * b : 128 * b + 128]
            return carry
        lax.fori_loop(a0, a1, one, 0)

    slot_a = [mail.slots(2), mail.slots(2)]
    slot_b = [mail.slots(4), mail.slots(4)]
    slot_c = [mail.slots(2), mail.slots(2)]
    slot_d = [mail.slots(4), mail.slots(4)]

    def rs1_start(j):
        am, ap, an = (u + 2) % 4, (u + 1) % 4, (u + 3) % 4
        lo, hi = pl.ds(0, 2), pl.ds(2, 2)
        mail.post(slot_a[j][0], p.at[j, am, lo], ra.at[j, 0], udev(1))
        mail.post(slot_a[j][1], p.at[j, am, hi], ra.at[j, 1], udev(-1))
        mail.post(slot_b[j][0], p.at[j, ap, hi], rb.at[j, 0, hi], udev(1))
        mail.post(slot_b[j][1], p.at[j, an, lo], rb.at[j, 1, lo], udev(-1))

    def rs1_mid(j):
        ap, an = (u + 1) % 4, (u + 3) % 4
        lo, hi = pl.ds(0, 2), pl.ds(2, 2)
        mail.take(slot_a[j][0], ra.at[j, 0], udev(1))
        ra[j, 0] += p[j, ap, 0:2]
        mail.post(slot_b[j][2], ra.at[j, 0], rb.at[j, 0, lo], udev(1))
        mail.take(slot_a[j][1], ra.at[j, 1], udev(-1))
        ra[j, 1] += p[j, an, 2:4]
        mail.post(slot_b[j][3], ra.at[j, 1], rb.at[j, 1, hi], udev(-1))

    def rs1_end(j):
        lo, hi = pl.ds(0, 2), pl.ds(2, 2)
        mail.take(slot_b[j][0], rb.at[j, 0, hi], udev(1))
        mail.take(slot_b[j][1], rb.at[j, 1, lo], udev(-1))
        mail.take(slot_b[j][2], rb.at[j, 0, lo], udev(1))
        mail.take(slot_b[j][3], rb.at[j, 1, hi], udev(-1))
        vm, vp, vn = (v + 2) % 4, (v + 1) % 4, (v + 3) % 4
        lo, hi = pl.ds(0, 96), pl.ds(96, 96)

        def add(b):
            s[j, b] = p[j, u, b] + rb[j, 0, b] + rb[j, 1, b]

        add(vm)
        mail.post(slot_c[j][0], s.at[j, vm, lo], sa.at[j, 0], vdev(1))
        mail.post(slot_c[j][1], s.at[j, vm, hi], sa.at[j, 1], vdev(-1))
        add(vp)
        mail.post(slot_d[j][0], s.at[j, vp, hi], sb.at[j, 0, hi], vdev(1))
        add(vn)
        mail.post(slot_d[j][1], s.at[j, vn, lo], sb.at[j, 1, lo], vdev(-1))
        add(v)

    def rs2_mid(j):
        vp, vn = (v + 1) % 4, (v + 3) % 4
        lo, hi = pl.ds(0, 96), pl.ds(96, 96)
        mail.take(slot_c[j][0], sa.at[j, 0], vdev(1))
        sa[j, 0] += s[j, vp, 0:96]
        mail.post(slot_d[j][2], sa.at[j, 0], sb.at[j, 0, lo], vdev(1))
        mail.take(slot_c[j][1], sa.at[j, 1], vdev(-1))
        sa[j, 1] += s[j, vn, 96:192]
        mail.post(slot_d[j][3], sa.at[j, 1], sb.at[j, 1, hi], vdev(-1))

    slot_i = [mail.slots(3), mail.slots(3)]
    slot_t = mail.slots(2)

    def rs2_end(j):
        lo, hi = pl.ds(0, 96), pl.ds(96, 96)
        mail.take(slot_d[j][0], sb.at[j, 0, hi], vdev(1))
        mail.take(slot_d[j][1], sb.at[j, 1, lo], vdev(-1))
        mail.take(slot_d[j][2], sb.at[j, 0, lo], vdev(1))
        mail.take(slot_d[j][3], sb.at[j, 1, hi], vdev(-1))
        got = s[j, v] + sb[j, 0] + sb[j, 1]
        tx[j, k] = got.reshape(4, 48, 128)
        mail.post(slot_t[j], tx.at[j, k], tx.at[j, k], partner)

    def rows_send(j):
        ib[j, y] = tx[j, k, y]
        for d in range(1, 4):
            mail.post(slot_i[j][d - 1], tx.at[j, k, (y + d) % 4], ib.at[j, y], ydev(d))

    def rows_take(j):
        for d in range(1, 4):
            mail.take(slot_i[j][d - 1], ib.at[j, (y + 4 - d) % 4], ydev(d))
        return jnp.concatenate([ib[j, b] for b in range(4)], axis=1)

    slot_fy = mail.slots(3)
    slot_ftx = mail.slots(1)[0]

    def mates_send():
        mail.take(slot_fx, fy.at[y, other], partner)
        for d in range(1, 4):
            mail.post(slot_fy[d - 1], fy.at[y], fy.at[y], ydev(d))

    def mates_take():
        for d in range(1, 4):
            mail.take(slot_fy[d - 1], fy.at[(y + 4 - d) % 4], ydev(d))
        for c in range(2):
            ft[:, 192 * c : 192 * c + 192] = jnp.concatenate([fy[b, c] for b in range(4)], axis=0).T

    def mates_half():
        copy = mail.desc(slot_ftx, ft.at[pl.ds(0, 256)], ftb, partner)
        pl.when(k == 1)(copy.start)

    def mates_half_take():
        copy = mail.desc(slot_ftx, ft.at[pl.ds(0, 256)], ftb, partner)
        pl.when(k == 0)(copy.wait_recv)
        pl.when(k == 1)(copy.wait_send)

        @pl.when(k == 1)
        def _():
            ftb[...] = ft[256:512]

    slot_x = [mail.slots(3), mail.slots(3)]
    slot_z = [mail.slots(7), mail.slots(7)]
    slot_gx = [mail.slots(3), mail.slots(3)]
    slot_gy = [mail.slots(3), mail.slots(3)]
    slot_gc = [mail.slots(4), mail.slots(4)]
    size = (128, 64)

    def cbr(j):
        return cb.at[j, :, pl.ds(0, size[j])]

    def cross(j):
        mail.take(slot_t[j], tx.at[j, other], partner)
        tt = halves(jnp.concatenate([tx[j, 0].reshape(192, 128), tx[j, 1].reshape(192, 128)], axis=0))
        left = ft[...] if j == 0 else ftb[...]
        got = dot3(halves(left), tt)
        n = size[j]
        for b in range(4):
            cb[j, b, 0:n] = got[n * b : n * b + n]
        for d in (2, 1, 3):
            mail.post(slot_x[j][d - 1], cb.at[j, (x + d) % 4, pl.ds(0, n)], cx.at[j, d - 1, pl.ds(0, n)], xdev(d))

    def cross_z(j):
        n = size[j]
        total = cb[j, x, 0:n]
        for d in range(1, 4):
            mail.take(slot_x[j][d - 1], cx.at[j, d - 1, pl.ds(0, n)], xdev(d))
            total += cx[j, d - 1, 0:n]
        cz[j, z, 0:n] = total
        for d in (4, 3, 5, 2, 6, 1, 7):
            mail.post(slot_z[j][d - 1], cz.at[j, z, pl.ds(0, n)], cz.at[j, z, pl.ds(0, n)], zdev(d))

    def cross_x(j):
        n = size[j]
        for d in range(1, 8):
            mail.take(slot_z[j][d - 1], cz.at[j, (z + 8 - d) % 8, pl.ds(0, n)], zdev(d))
        total = cz[j, 0, 0:n]
        for b in range(1, 8):
            total += cz[j, b, 0:n]
        piece = cf.at[j, k, y, x, pl.ds(0, n)]
        piece[...] = total
        for d in (2, 1, 3):
            mail.post(slot_gx[j][d - 1], piece, piece, xdev(d))

    def cross_y(j):
        n = size[j]
        for d in range(1, 4):
            mail.take(slot_gx[j][d - 1], cf.at[j, k, y, (x + 4 - d) % 4, pl.ds(0, n)], xdev(d))
        piece = cf.at[j, k, y, :, pl.ds(0, n)]
        for d in (2, 1, 3):
            mail.post(slot_gy[j][d - 1], piece, piece, ydev(d))
        mail.post(slot_gc[j][0], piece, piece, partner)

    def cross_c(j):
        n = size[j]
        for d in (1, 3, 2):
            piece = cf.at[j, k, (y + 4 - d) % 4, :, pl.ds(0, n)]
            mail.take(slot_gy[j][d - 1], piece, ydev(d))
            mail.post(slot_gc[j][d], piece, piece, partner)

    def cross_end(j):
        n = size[j]
        for d in range(4):
            mail.take(slot_gc[j][d], cf.at[j, other, (y + 4 - d) % 4, :, pl.ds(0, n)], partner)

    for c in load_r:
        c.wait()
    split_r(0, k)
    ring(0, 0)
    for a in range(4):
        mail.take(slot_r[a], rx.at[other, a], partner)
    ring(0, 1)
    split_r(1, other)
    collect(0, 0)
    mates_send()
    ring(0, 2)
    collect(0, 1)
    ring(0, 3)
    ring(1, 0)
    collect(0, 2)
    ring(0, 4)
    ring(1, 1)
    collect(0, 3)
    collect(0, 4)
    product(0, 0, 2)
    ring(1, 2)
    product(0, 2, 4)
    rs1_start(0)
    collect(1, 0)
    ring(1, 3)
    collect(1, 1)
    rs1_mid(0)
    ring(1, 4)
    for st in (2, 3, 4):
        collect(1, st)
    product(1, 0, 4)
    rs1_start(1)
    rs1_end(0)
    mates_take()
    mates_half()
    rs1_mid(1)
    rs2_mid(0)
    rs2_end(0)
    rows_send(0)
    cross(0)
    rs1_end(1)
    cross_z(0)
    load_k.wait()
    kh = halves(kk_v[...])
    t_own = rows_take(0)
    o1[...] = -t_own
    out1 = here(o1, inv1_o)
    t_coup = dot3(halves(t_own), kh)
    rs2_mid(1)
    mates_half_take()
    rs2_end(1)
    rows_send(1)
    cross(1)
    cross_x(0)
    cross_z(1)
    cross_y(0)
    cross_c(0)
    cross_x(1)
    cross_end(0)
    o2[...] = t_coup - rows_take(1)
    out2 = here(o2, inv2_o)
    load_d1.wait()
    load_d2.wait()
    c11 = jnp.concatenate([cf[0, 0, b].reshape(W, 128) for b in range(4)], axis=1)
    ob1[...] = d1_v[...] + c11
    out3 = here(ob1, blk1_o)
    c21 = jnp.concatenate([cf[0, 1, b].reshape(W, 128) for b in range(4)], axis=1)
    oc[...] = c21.T - dot3(halves(ob1[...]), kh)
    out4 = here(oc, cpl_o)
    cross_y(1)
    c21 = jnp.concatenate([cf[0, 1, b].reshape(W, 128) for b in range(4)], axis=1)
    kh = halves(kk_v[...])
    kt = halves(kk_v[...].T)
    ob2[...] = d2_v[...] - dot3(halves(c21), kh) - dot3(kt, halves(oc[...]))
    cross_c(1)
    cross_end(1)
    for c in range(2):
        for b in range(4):
            ob2[256 * c : 256 * c + 256, 128 * b : 128 * b + 128] += cf[1, c, b, :, 0:64].reshape(256, 128)
    out5 = here(ob2, blk2_o)
    for copy in mail.sent:
        copy.wait_send()
    for copy in (out1, out2, out3, out4, out5):
        copy.wait()


def body(resident, factor_one, pattern_one, factor_two, pattern_two, coupling, diagonal_one, diagonal_two):
    tiles = resident.reshape(4, 4, 2, 48, 384)
    vm = pltpu.VMEM
    any_ = pl.BlockSpec(memory_space=pl.ANY)
    smem = pl.BlockSpec(memory_space=pltpu.SMEM)
    sds = jax.ShapeDtypeStruct
    return pl.pallas_call(
        kernel,
        out_shape=(sds((48, W), F32), sds((W, W), F32), sds((48, W), F32), sds((W, W), F32), sds((W, W), F32)),
        in_specs=[any_, any_, smem, any_, smem, any_, any_, any_],
        out_specs=(any_,) * 5,
        scratch_shapes=[
            vm((2, 48, W), F32),
            vm((2, 4, 4, 48, 384), F32),
            vm((4, 192, 768), BF),
            vm((4, 192, 768), BF),
            vm((2, 16, 48, W), F32),
            vm((2, 16, 48, W), BF),
            vm((2, 16, 48, W), BF),
            vm((2, 4, 4, 192, 128), F32),
            vm((2, 2, 2, 192, 128), F32),
            vm((2, 2, 4, 192, 128), F32),
            vm((2, 4, 192, 128), F32),
            vm((2, 2, 96, 128), F32),
            vm((2, 2, 192, 128), F32),
            vm((8, 128), F32),
            vm((2, 4, 48, 128), F32),
            vm((2, 2, 4, 48, 128), F32),
            vm((4, 2, 48, W), F32),
            vm((W, 384), F32),
            vm((256, 384), F32),
            vm((8, 128), F32),
            vm((2, 4, 128, 128), F32),
            vm((2, 3, 128, 128), F32),
            vm((2, 8, 128, 128), F32),
            vm((2, 2, 4, 4, 128, 128), F32),
            vm((W, W), F32),
            vm((W, W), F32),
            vm((W, W), F32),
            vm((48, W), F32),
            vm((48, W), F32),
            vm((W, W), F32),
            vm((W, W), F32),
            vm((W, W), F32),
            pltpu.SemaphoreType.DMA((N_MAIL,)),
            pltpu.SemaphoreType.DMA((N_MAIL,)),
            pltpu.SemaphoreType.DMA((N_LOCAL,)),
        ],
        name="selected_inverse",
        compiler_params=pltpu.CompilerParams(
            collective_id=0, has_side_effects=True, vmem_limit_bytes=52 << 20
        ),
        cost_estimate=pl.CostEstimate(flops=4_000_000_000, bytes_accessed=8_000_000, transcendentals=0),
    )(tiles, factor_one, pattern_one, factor_two, pattern_two, coupling, diagonal_one, diagonal_two)


def solution(mesh):
    return jax.shard_map(
        body,
        mesh=mesh,
        in_specs=(
            P("row", "col"),
            P(("row", "col"), None),
            P(("row", "col")),
            P(("row", "col"), None),
            P(("row", "col")),
            P(),
            P(),
            P(),
        ),
        out_specs=(P(("row", "col"), None), P(), P(("row", "col"), None), P(), P()),
        check_vma=False,
    )
```

```python
import jax
import jax.numpy as jnp
from jax import lax
from jax.experimental import pallas as pl
from jax.experimental.pallas import tpu as pltpu
from jax.sharding import PartitionSpec as P

W = 512
MESH = pl.DeviceIdType.MESH
BF = jnp.bfloat16
F32 = jnp.float32


def halves(value):
    high = value.astype(BF)
    return high, (value - high.astype(F32)).astype(BF)


def dot3(left, right):
    (lh, ll), (rh, rl) = left, right
    total = jnp.dot(lh, rh, preferred_element_type=F32)
    total += jnp.dot(lh, rl, preferred_element_type=F32)
    return total + jnp.dot(ll, rh, preferred_element_type=F32)


class Mail:
    def __init__(self, send, recv):
        self.send, self.recv, self.count, self.sent = send, recv, 0, []

    def slots(self, n):
        first = self.count
        self.count += n
        return list(range(first, first + n))

    def desc(self, slot, src, dst, dev):
        return pltpu.make_async_remote_copy(
            src, dst, self.send.at[slot], self.recv.at[slot], device_id=dev, device_id_type=MESH
        )

    def post(self, slot, src, dst, dev):
        copy = self.desc(slot, src, dst, dev)
        copy.start()
        self.sent.append(copy)

    def take(self, slot, dst, dev):
        self.desc(slot, dst, dst, dev).wait_recv()


N_MAIL = 200
N_LOCAL = 40
VMEM_LIMIT = 60 << 20


def kernel(
    res, fac1, pat1, fac2, pat2, coup, diag1, diag2,
    inv1_o, blk1_o, inv2_o, cpl_o, blk2_o,
    pat, own, rx, rh, rl, g, gh, gl, p, ra, rb, s, sb, ib, tx, fy, ft, ftb,
    cb, cx, ct, cz, wide, cf, kk_v, kb, d1_v, d2_v, o1, o2, ob1, ob2, oc,
    send, recv, local,
):
    z = lax.axis_index("row")
    col = lax.axis_index("col")
    k = col % 2
    x = (col // 2) % 4
    y = col // 8
    other = 1 - k

    def at(xx, yy, zz, kk):
        return (zz, (yy * 4 + xx) * 2 + kk)

    partner = at(x, y, z, other)

    def zdev(d):
        return at(x, y, (z + d + 8) % 8, k)

    def xdev(d):
        return at((x + d + 4) % 4, y, z, k)

    def ydev(d):
        return at(x, (y + d + 4) % 4, z, k)

    u = x + k * (y - x)
    v = y + k * (x - y)

    def udev(d):
        return at((x + (1 - k) * d + 4) % 4, (y + k * d + 4) % 4, z, k)

    def vdev(d):
        return at((x + k * d + 4) % 4, (y + (1 - k) * d + 4) % 4, z, k)

    goal = 2 * z + y // 2
    mine = (y % 2) * 4 + x
    target = at(goal % 4, goal // 4, (mine + 3 * z + 1) % 8, k)
    q = 4 * y + x
    z0 = q // 2
    chunks = {d: (z + d + 63 - 3 * z0) % 8 for d in range(-3, 5)}

    def chunk(d):
        return chunks[(d + 3) % 8 - 3]

    source = at(chunk(0) % 4, 2 * (q % 2) + chunk(0) // 4, z0, k)

    mail = Mail(send, recv)
    used = [0]

    def here(src, dst):
        copy = pltpu.make_async_copy(src, dst, local.at[used[0]])
        used[0] += 1
        copy.start()
        return copy

    load_p = [here(pat1, pat.at[0]), here(pat2, pat.at[1])]
    load_f = [here(fac1, own.at[0]), here(fac2, own.at[1])]
    load_r = [here(res.at[:, a, k], rx.at[k, a]) for a in range(4)]
    load_k = here(coup, kk_v)
    load_d1 = here(diag1, d1_v)
    load_d2 = here(diag2, d2_v)

    barrier = pltpu.get_barrier_semaphore()
    friends = [partner] + [zdev(d) for d in range(1, 8)] + [xdev(d) for d in range(1, 4)] + [ydev(d) for d in range(1, 4)]
    for dev in friends + [source]:
        pl.semaphore_signal(barrier, inc=1, device_id=dev, device_id_type=MESH)

    for j in range(2):
        load_p[j].wait()
        load_f[j].wait()
        for b in range(3):
            own[j, 16 * b : 16 * b + 16] = own[j, 16 * b : 16 * b + 16] * pat[j, b].astype(F32)
    pl.semaphore_wait(barrier, len(friends) + 1)

    slot_perm = mail.slots(2)
    slot_r = mail.slots(4)
    slot_fx = mail.slots(1)[0]

    def rows_to_column(j):
        mail.post(slot_perm[j], own.at[j], g.at[j, 2 * mine + k], target)

    def tiles_to_partner():
        for a in range(4):
            mail.post(slot_r[a], res.at[:, a, other], rx.at[k, a], partner)

    def tiles_take():
        for a in range(4):
            mail.take(slot_r[a], rx.at[other, a], partner)

    def rows_to_partner():
        fy[y, k] = own[k]
        mail.post(slot_fx, own.at[other], fy.at[y, k], partner)

    slot_up = [mail.slots(4), mail.slots(4)]
    slot_dn = [mail.slots(4), mail.slots(4)]
    slot_fwd = [mail.slots(8), mail.slots(8)]

    def split(j, m):
        gh[j, m], gl[j, m] = halves(g[j, m])

    def forward(j, f, d):
        m = 2 * chunk(d) + k
        mail.post(slot_fwd[j][f], g.at[j, m], g.at[j, m], partner)
        split(j, m)

    def arrived(j, f, d):
        m = 2 * chunk(d) + other
        mail.take(slot_fwd[j][f], g.at[j, m], partner)
        split(j, m)

    def ring(j, step):
        m_up = 2 * chunk(-step) + k
        m_dn = 2 * chunk(step) + k
        if step == 0:
            mail.take(slot_perm[j], g.at[j, m_up], target)
            mail.post(slot_up[j][0], g.at[j, m_up], g.at[j, m_up], zdev(1))
            mail.post(slot_dn[j][0], g.at[j, m_up], g.at[j, m_up], zdev(-1))
            forward(j, 0, 0)
            return
        lo = g.at[j, m_up]
        hi = g.at[j, m_dn]
        if step == 4:
            mail.take(slot_up[j][3], lo.at[pl.ds(0, 24)], zdev(1))
            mail.take(slot_dn[j][3], hi.at[pl.ds(24, 24)], zdev(-1))
            forward(j, 7, 4)
            return
        mail.take(slot_up[j][step - 1], g.at[j, m_up], zdev(1))
        if step == 3:
            mail.post(slot_up[j][3], lo.at[pl.ds(0, 24)], lo.at[pl.ds(0, 24)], zdev(1))
        else:
            mail.post(slot_up[j][step], lo, lo, zdev(1))
        mail.take(slot_dn[j][step - 1], g.at[j, m_dn], zdev(-1))
        if step == 3:
            mail.post(slot_dn[j][3], hi.at[pl.ds(24, 24)], hi.at[pl.ds(24, 24)], zdev(-1))
        else:
            mail.post(slot_dn[j][step], hi, hi, zdev(-1))
        forward(j, 2 * step - 1, -step)
        forward(j, 2 * step, step)

    def collect(j, step):
        if step in (0, 4):
            arrived(j, 0 if step == 0 else 7, step)
        else:
            arrived(j, 2 * step - 1, -step)
            arrived(j, 2 * step, step)

    def split_r(dyn):
        for a in range(4):
            hi, lo = halves(rx[dyn, a].reshape(192, 384))
            rh[a, :, pl.ds(pl.multiple_of(dyn * 384, 128), 384)] = hi
            rl[a, :, pl.ds(pl.multiple_of(dyn * 384, 128), 384)] = lo

    def product(j):
        tiles = (rh[...].reshape(768, 768), rl[...].reshape(768, 768))
        got = dot3(tiles, (gh[j].reshape(768, W), gl[j].reshape(768, W)))
        for a in range(4):
            for b in range(4):
                p[j, a + k * (b - a), b + k * (a - b)] = got[192 * a : 192 * a + 192, 128 * b : 128 * b + 128]

    slot_a = [mail.slots(2), mail.slots(2)]
    slot_b = [mail.slots(4), mail.slots(4)]
    slot_d = [mail.slots(3), mail.slots(3)]

    def rs1_start(j):
        am, ap, an = (u + 2) % 4, (u + 1) % 4, (u + 3) % 4
        lo, hi = pl.ds(0, 2), pl.ds(2, 2)
        mail.post(slot_a[j][0], p.at[j, am, lo], ra.at[j, 0], udev(1))
        mail.post(slot_a[j][1], p.at[j, am, hi], ra.at[j, 1], udev(-1))
        mail.post(slot_b[j][0], p.at[j, ap, hi], rb.at[j, 0, hi], udev(1))
        mail.post(slot_b[j][1], p.at[j, an, lo], rb.at[j, 1, lo], udev(-1))

    def rs1_mid(j):
        ap, an = (u + 1) % 4, (u + 3) % 4
        lo, hi = pl.ds(0, 2), pl.ds(2, 2)
        mail.take(slot_a[j][0], ra.at[j, 0], udev(1))
        ra[j, 0] += p[j, ap, 0:2]
        mail.post(slot_b[j][2], ra.at[j, 0], rb.at[j, 0, lo], udev(1))
        mail.take(slot_a[j][1], ra.at[j, 1], udev(-1))
        ra[j, 1] += p[j, an, 2:4]
        mail.post(slot_b[j][3], ra.at[j, 1], rb.at[j, 1, hi], udev(-1))

    def rs1_end(j):
        lo, hi = pl.ds(0, 2), pl.ds(2, 2)
        mail.take(slot_b[j][0], rb.at[j, 0, hi], udev(1))
        mail.take(slot_b[j][1], rb.at[j, 1, lo], udev(-1))
        mail.take(slot_b[j][2], rb.at[j, 0, lo], udev(1))
        mail.take(slot_b[j][3], rb.at[j, 1, hi], udev(-1))
        for d in (2, 1, 3, 0):
            b = (v + d) % 4
            s[j, b] = p[j, u, b] + rb[j, 0, b] + rb[j, 1, b]
            if d:
                mail.post(slot_d[j][d - 1], s.at[j, b], sb.at[j, d - 1], vdev(d))

    slot_i = [mail.slots(3), mail.slots(3)]
    slot_t = mail.slots(2)

    def rs2_end(j):
        for d in range(1, 4):
            mail.take(slot_d[j][d - 1], sb.at[j, d - 1], vdev(d))
        got = s[j, v] + sb[j, 0] + sb[j, 1] + sb[j, 2]
        tx[j, k] = got.reshape(4, 48, 128)
        mail.post(slot_t[j], tx.at[j, k], tx.at[j, k], partner)

    def rows_send(j):
        ib[j, y] = tx[j, k, y]
        for d in range(1, 4):
            mail.post(slot_i[j][d - 1], tx.at[j, k, (y + d) % 4], ib.at[j, y], ydev(d))

    def rows_take(j):
        for d in range(1, 4):
            mail.take(slot_i[j][d - 1], ib.at[j, (y + 4 - d) % 4], ydev(d))
        return jnp.concatenate([ib[j, b] for b in range(4)], axis=1)

    slot_fy = mail.slots(3)
    slot_ftx = mail.slots(1)[0]

    def mates_send():
        mail.take(slot_fx, fy.at[y, other], partner)
        for d in range(1, 4):
            mail.post(slot_fy[d - 1], fy.at[y], fy.at[y], ydev(d))

    def mates_take():
        for d in range(1, 4):
            mail.take(slot_fy[d - 1], fy.at[(y + 4 - d) % 4], ydev(d))
        for c in range(2):
            ft[:, 192 * c : 192 * c + 192] = jnp.concatenate([fy[b, c] for b in range(4)], axis=0).T

    def mates_half():
        copy = mail.desc(slot_ftx, ft.at[pl.ds(0, 256)], ftb, partner)
        pl.when(k == 1)(copy.start)

    def mates_half_take():
        copy = mail.desc(slot_ftx, ft.at[pl.ds(0, 256)], ftb, partner)
        pl.when(k == 0)(copy.wait_recv)
        pl.when(k == 1)(copy.wait_send)

        @pl.when(k == 1)
        def _():
            ftb[...] = ft[256:512]

    slot_x = [mail.slots(3), mail.slots(3)]
    slot_z = [mail.slots(7), mail.slots(7)]
    slot_gz = [mail.slots(7), mail.slots(7)]
    slot_gu = [mail.slots(3), mail.slots(3)]
    slot_gv = [mail.slots(3), mail.slots(3)]
    slot_gc = [mail.slots(4), mail.slots(4)]
    size = (128, 64)

    def cross(j):
        mail.take(slot_t[j], tx.at[j, other], partner)
        tt = halves(jnp.concatenate([tx[j, 0].reshape(192, 128), tx[j, 1].reshape(192, 128)], axis=0))
        left = ft[...] if j == 0 else ftb[...]
        got = dot3(halves(left), tt)
        n = size[j]
        for b in range(4):
            cb[j, b, 0:n] = got[n * b : n * b + n]
        for d in (2, 1, 3):
            mail.post(slot_x[j][d - 1], cb.at[j, (x + d) % 4, pl.ds(0, n)], cx.at[j, d - 1, pl.ds(0, n)], xdev(d))

    def cross_x(j):
        n, e = size[j], size[j] // 8
        total = cb[j, x, 0:n]
        for d in range(1, 4):
            mail.take(slot_x[j][d - 1], cx.at[j, d - 1, pl.ds(0, n)], xdev(d))
            total += cx[j, d - 1, 0:n]
        if j == 1:
            wide[z] = total
            for d in (4, 3, 5, 2, 6, 1, 7):
                mail.post(slot_z[j][d - 1], wide.at[z], wide.at[z], zdev(d))
            return
        for b in range(8):
            ct[j, b, 0:e] = total[e * b : e * b + e]
        for d in (4, 3, 5, 2, 6, 1, 7):
            mail.post(slot_z[j][d - 1], ct.at[j, (z + d) % 8, pl.ds(0, e)], cz.at[j, d - 1, pl.ds(0, e)], zdev(d))

    def cross_z(j):
        e = size[j] // 8
        total = ct[j, z, 0:e]
        for d in range(1, 8):
            mail.take(slot_z[j][d - 1], cz.at[j, d - 1, pl.ds(0, e)], zdev(d))
            total += cz[j, d - 1, 0:e]
        piece = cf.at[j, k, v, u, z, pl.ds(0, e)]
        piece[...] = total
        for d in (4, 3, 5, 2, 6, 1, 7):
            mail.post(slot_gz[j][d - 1], piece, piece, zdev(d))

    def cross_u(j):
        e = size[j] // 8
        if j == 1:
            for d in range(1, 8):
                mail.take(slot_z[j][d - 1], wide.at[(z + 8 - d) % 8], zdev(d))
            total = wide[0]
            for b in range(1, 8):
                total += wide[b]
            cf[j, k, v, u, :, 0:e] = total.reshape(8, e, 128)
        else:
            for d in range(1, 8):
                mail.take(slot_gz[j][d - 1], cf.at[j, k, v, u, (z + 8 - d) % 8, pl.ds(0, e)], zdev(d))
        piece = cf.at[j, k, v, u, :, pl.ds(0, e)]
        for d in (2, 1, 3):
            mail.post(slot_gu[j][d - 1], piece, piece, udev(d))

    def cross_v(j):
        e = size[j] // 8
        for d in range(1, 4):
            mail.take(slot_gu[j][d - 1], cf.at[j, k, v, (u + 4 - d) % 4, :, pl.ds(0, e)], udev(d))
        piece = cf.at[j, k, v, :, :, pl.ds(0, e)]
        for d in (2, 1, 3):
            mail.post(slot_gv[j][d - 1], piece, piece, vdev(d))
        mail.post(slot_gc[j][0], piece, piece, partner)

    def cross_c(j):
        e = size[j] // 8
        for d in (1, 3, 2):
            piece = cf.at[j, k, (v + 4 - d) % 4, :, :, pl.ds(0, e)]
            mail.take(slot_gv[j][d - 1], piece, vdev(d))
            mail.post(slot_gc[j][d], piece, piece, partner)

    def cross_end(j):
        e = size[j] // 8
        for d in range(4):
            mail.take(slot_gc[j][d], cf.at[j, other, (u + 4 - d) % 4, :, :, pl.ds(0, e)], partner)

    def whole(c):
        parts = []
        for b in range(4):
            if c == 0:
                parts.append(cf[0, 0, b].reshape(W, 128))
            else:
                parts.append(cf[0, 1, :, b].reshape(W, 128))
        return jnp.concatenate(parts, axis=1)

    rows_to_column(0)
    rows_to_column(1)
    tiles_to_partner()
    rows_to_partner()
    for c in load_r:
        c.wait()
    split_r(k)
    ring(0, 0)
    ring(1, 0)
    mates_send()
    tiles_take()
    split_r(other)
    ring(0, 1)
    ring(1, 1)
    collect(0, 0)
    collect(1, 0)
    ring(0, 2)
    ring(1, 2)
    collect(0, 1)
    collect(1, 1)
    ring(0, 3)
    ring(1, 3)
    collect(0, 2)
    collect(1, 2)
    ring(0, 4)
    collect(0, 3)
    collect(0, 4)
    product(0)
    rs1_start(0)
    ring(1, 4)
    collect(1, 3)
    collect(1, 4)
    product(1)
    rs1_start(1)
    rs1_mid(0)
    mates_take()
    mates_half()
    rs1_mid(1)
    load_k.wait()
    kb[0], kb[1] = halves(kk_v[...])
    kb[2], kb[3] = halves(kk_v[...].T)
    rs1_end(0)
    mates_half_take()
    rs1_end(1)
    rs2_end(0)
    rows_send(0)
    cross(0)
    rs2_end(1)
    rows_send(1)
    cross_x(0)
    cross(1)
    cross_z(0)
    cross_x(1)
    t_own = rows_take(0)
    o1[...] = -t_own
    out1 = here(o1, inv1_o)
    o2[...] = dot3(halves(t_own), (kb[0], kb[1])) - rows_take(1)
    out2 = here(o2, inv2_o)
    cross_u(0)
    cross_v(0)
    cross_u(1)
    cross_c(0)
    cross_v(1)
    cross_end(0)
    load_d1.wait()
    load_d2.wait()
    ob1[...] = d1_v[...] + whole(0)
    out3 = here(ob1, blk1_o)
    c21 = whole(1)
    oc[...] = c21.T - dot3(halves(ob1[...]), (kb[0], kb[1]))
    out4 = here(oc, cpl_o)
    ob2[...] = d2_v[...] - dot3(halves(c21), (kb[0], kb[1])) - dot3((kb[2], kb[3]), halves(oc[...]))
    cross_c(1)
    cross_end(1)
    for b in range(4):
        for a in range(4):
            cols = slice(128 * b, 128 * b + 128)
            ob2[64 * a : 64 * a + 64, cols] += cf[1, 0, b, a, :, 0:8].reshape(64, 128)
            ob2[256 + 64 * a : 320 + 64 * a, cols] += cf[1, 1, a, b, :, 0:8].reshape(64, 128)
    out5 = here(ob2, blk2_o)
    for copy in mail.sent:
        copy.wait_send()
    for copy in (out1, out2, out3, out4, out5):
        copy.wait()


def place_kernel(*refs):
    held, sem = refs[10:15], refs[15]
    loads = [pltpu.make_async_copy(refs[i], held[i], sem.at[i]) for i in range(5)]
    stores = [pltpu.make_async_copy(held[i], refs[5 + i], sem.at[5 + i]) for i in range(5)]
    for copy in loads:
        copy.start()
    for load, store in zip(loads, stores):
        load.wait()
        store.start()
    for copy in stores:
        copy.wait()


def body(resident, factor_one, pattern_one, factor_two, pattern_two, coupling, diagonal_one, diagonal_two):
    tiles = resident.reshape(4, 4, 2, 48, 384)
    vm = pltpu.VMEM
    any_ = pl.BlockSpec(memory_space=pltpu.HBM)
    sds = jax.ShapeDtypeStruct
    shapes = (sds((48, W), F32), sds((W, W), F32), sds((48, W), F32), sds((W, W), F32), sds((W, W), F32))
    results = pl.pallas_call(
        kernel,
        out_shape=shapes,
        in_specs=[any_] * 8,
        out_specs=(any_,) * 5,
        scratch_shapes=[
            pltpu.SMEM((2, 3), jnp.int32),
            vm((2, 48, W), F32),
            vm((2, 4, 4, 48, 384), F32),
            vm((4, 192, 768), BF),
            vm((4, 192, 768), BF),
            vm((2, 16, 48, W), F32),
            vm((2, 16, 48, W), BF),
            vm((2, 16, 48, W), BF),
            vm((2, 4, 4, 192, 128), F32),
            vm((2, 2, 2, 192, 128), F32),
            vm((2, 2, 4, 192, 128), F32),
            vm((2, 4, 192, 128), F32),
            vm((2, 3, 192, 128), F32),
            vm((2, 4, 48, 128), F32),
            vm((2, 2, 4, 48, 128), F32),
            vm((4, 2, 48, W), F32),
            vm((W, 384), F32),
            vm((256, 384), F32),
            vm((2, 4, 128, 128), F32),
            vm((2, 3, 128, 128), F32),
            vm((2, 8, 16, 128), F32),
            vm((2, 7, 16, 128), F32),
            vm((8, 64, 128), F32),
            vm((2, 2, 4, 4, 8, 16, 128), F32),
            vm((W, W), F32),
            vm((4, W, W), BF),
            vm((W, W), F32),
            vm((W, W), F32),
            vm((48, W), F32),
            vm((48, W), F32),
            vm((W, W), F32),
            vm((W, W), F32),
            vm((W, W), F32),
            pltpu.SemaphoreType.DMA((N_MAIL,)),
            pltpu.SemaphoreType.DMA((N_MAIL,)),
            pltpu.SemaphoreType.DMA((N_LOCAL,)),
        ],
        name="selected_inverse",
        compiler_params=pltpu.CompilerParams(
            collective_id=0, has_side_effects=True, vmem_limit_bytes=VMEM_LIMIT
        ),
        cost_estimate=pl.CostEstimate(flops=4_000_000_000, bytes_accessed=8_000_000, transcendentals=0),
    )(tiles, factor_one, pattern_one, factor_two, pattern_two, coupling, diagonal_one, diagonal_two)
    free = pl.BlockSpec(memory_space=pl.ANY)
    return pl.pallas_call(
        place_kernel,
        out_shape=shapes,
        in_specs=[free] * 5,
        out_specs=(free,) * 5,
        scratch_shapes=[vm(shape.shape, F32) for shape in shapes] + [pltpu.SemaphoreType.DMA((10,))],
        name="place_results",
    )(*results)


def solution(mesh):
    return jax.shard_map(
        body,
        mesh=mesh,
        in_specs=(
            P("row", "col"),
            P(("row", "col"), None),
            P(("row", "col")),
            P(("row", "col"), None),
            P(("row", "col")),
            P(),
            P(),
            P(),
        ),
        out_specs=(P(("row", "col"), None), P(), P(("row", "col"), None), P(), P()),
        check_vma=False,
    )
```

```python
import jax
import jax.numpy as jnp
from jax import lax
from jax.experimental import pallas as pl
from jax.experimental.pallas import tpu as pltpu
from jax.sharding import PartitionSpec as P

W = 512
MESH = pl.DeviceIdType.MESH
BF = jnp.bfloat16
F32 = jnp.float32


def halves(value):
    high = value.astype(BF)
    return high, (value - high.astype(F32)).astype(BF)


def dot3(left, right):
    (lh, ll), (rh, rl) = left, right
    total = jnp.dot(lh, rh, preferred_element_type=F32)
    total += jnp.dot(lh, rl, preferred_element_type=F32)
    return total + jnp.dot(ll, rh, preferred_element_type=F32)


class Mail:
    def __init__(self, send, recv):
        self.send, self.recv, self.count, self.sent = send, recv, 0, []

    def slots(self, n):
        first = self.count
        self.count += n
        return list(range(first, first + n))

    def desc(self, slot, src, dst, dev):
        return pltpu.make_async_remote_copy(
            src, dst, self.send.at[slot], self.recv.at[slot], device_id=dev, device_id_type=MESH
        )

    def post(self, slot, src, dst, dev):
        copy = self.desc(slot, src, dst, dev)
        copy.start()
        self.sent.append(copy)

    def take(self, slot, dst, dev):
        self.desc(slot, dst, dst, dev).wait_recv()


N_MAIL = 200
N_LOCAL = 40
VMEM_LIMIT = 60 << 20


def kernel(
    res, fac1, pat1, fac2, pat2, coup, diag1, diag2,
    inv1_o, blk1_o, inv2_o, cpl_o, blk2_o,
    pat, own, rx, rh, rl, g, gh, gl, p, ra, rb, s, sb, ib, tx, fy, ft, ftb,
    cb, cx, ct, cz, cf, kk_v, kb, d1_v, d2_v, o1, o2, ob1, ob2, oc,
    send, recv, local,
):
    z = lax.axis_index("row")
    col = lax.axis_index("col")
    k = col % 2
    x = (col // 2) % 4
    y = col // 8
    other = 1 - k

    def at(xx, yy, zz, kk):
        return (zz, (yy * 4 + xx) * 2 + kk)

    partner = at(x, y, z, other)

    def zdev(d):
        return at(x, y, (z + d + 8) % 8, k)

    def xdev(d):
        return at((x + d + 4) % 4, y, z, k)

    def ydev(d):
        return at(x, (y + d + 4) % 4, z, k)

    u = x + k * (y - x)
    v = y + k * (x - y)

    def udev(d):
        return at((x + (1 - k) * d + 4) % 4, (y + k * d + 4) % 4, z, k)

    def vdev(d):
        return at((x + k * d + 4) % 4, (y + (1 - k) * d + 4) % 4, z, k)

    goal = 2 * z + y // 2
    mine = (y % 2) * 4 + x
    target = at(goal % 4, goal // 4, (mine + 3 * z + 1) % 8, k)
    q = 4 * y + x
    z0 = q // 2
    chunks = {d: (z + d + 63 - 3 * z0) % 8 for d in range(-3, 5)}

    def chunk(d):
        return chunks[(d + 3) % 8 - 3]

    source = at(chunk(0) % 4, 2 * (q % 2) + chunk(0) // 4, z0, k)

    mail = Mail(send, recv)
    used = [0]

    def here(src, dst):
        copy = pltpu.make_async_copy(src, dst, local.at[used[0]])
        used[0] += 1
        copy.start()
        return copy

    load_p = [here(pat1, pat.at[0]), here(pat2, pat.at[1])]
    load_f = [here(fac1, own.at[0]), here(fac2, own.at[1])]
    load_r = [here(res.at[:, a, k], rx.at[k, a]) for a in range(4)]
    load_k = here(coup, kk_v)
    load_d1 = here(diag1, d1_v)
    load_d2 = here(diag2, d2_v)

    barrier = pltpu.get_barrier_semaphore()
    friends = [partner] + [zdev(d) for d in range(1, 8)] + [xdev(d) for d in range(1, 4)] + [ydev(d) for d in range(1, 4)]
    for dev in friends + [source]:
        pl.semaphore_signal(barrier, inc=1, device_id=dev, device_id_type=MESH)

    for j in range(2):
        load_p[j].wait()
        load_f[j].wait()
        for b in range(3):
            own[j, 16 * b : 16 * b + 16] = own[j, 16 * b : 16 * b + 16] * pat[j, b].astype(F32)
    pl.semaphore_wait(barrier, len(friends) + 1)

    slot_perm = mail.slots(2)
    slot_r = mail.slots(4)
    slot_fx = mail.slots(1)[0]

    def rows_to_column(j):
        mail.post(slot_perm[j], own.at[j], g.at[j, 2 * mine + k], target)

    def tiles_to_partner():
        for a in range(4):
            mail.post(slot_r[a], res.at[:, a, other], rx.at[k, a], partner)

    def tiles_take():
        for a in range(4):
            mail.take(slot_r[a], rx.at[other, a], partner)

    def rows_to_partner():
        fy[y, k] = own[k]
        mail.post(slot_fx, own.at[other], fy.at[y, k], partner)

    slot_up = [mail.slots(4), mail.slots(4)]
    slot_dn = [mail.slots(4), mail.slots(4)]
    slot_fwd = [mail.slots(8), mail.slots(8)]

    def split(j, m):
        gh[j, m], gl[j, m] = halves(g[j, m])

    def forward(j, f, d):
        m = 2 * chunk(d) + k
        mail.post(slot_fwd[j][f], g.at[j, m], g.at[j, m], partner)
        split(j, m)

    def arrived(j, f, d):
        m = 2 * chunk(d) + other
        mail.take(slot_fwd[j][f], g.at[j, m], partner)
        split(j, m)

    def ring(j, step):
        m_up = 2 * chunk(-step) + k
        m_dn = 2 * chunk(step) + k
        if step == 0:
            mail.take(slot_perm[j], g.at[j, m_up], target)
            mail.post(slot_up[j][0], g.at[j, m_up], g.at[j, m_up], zdev(1))
            mail.post(slot_dn[j][0], g.at[j, m_up], g.at[j, m_up], zdev(-1))
            forward(j, 0, 0)
            return
        lo = g.at[j, m_up]
        hi = g.at[j, m_dn]
        if step == 4:
            mail.take(slot_up[j][3], lo.at[pl.ds(0, 24)], zdev(1))
            mail.take(slot_dn[j][3], hi.at[pl.ds(24, 24)], zdev(-1))
            forward(j, 7, 4)
            return
        mail.take(slot_up[j][step - 1], g.at[j, m_up], zdev(1))
        if step == 3:
            mail.post(slot_up[j][3], lo.at[pl.ds(0, 24)], lo.at[pl.ds(0, 24)], zdev(1))
        else:
            mail.post(slot_up[j][step], lo, lo, zdev(1))
        mail.take(slot_dn[j][step - 1], g.at[j, m_dn], zdev(-1))
        if step == 3:
            mail.post(slot_dn[j][3], hi.at[pl.ds(24, 24)], hi.at[pl.ds(24, 24)], zdev(-1))
        else:
            mail.post(slot_dn[j][step], hi, hi, zdev(-1))
        forward(j, 2 * step - 1, -step)
        forward(j, 2 * step, step)

    def collect(j, step):
        if step in (0, 4):
            arrived(j, 0 if step == 0 else 7, step)
        else:
            arrived(j, 2 * step - 1, -step)
            arrived(j, 2 * step, step)

    def split_r(dyn):
        for a in range(4):
            hi, lo = halves(rx[dyn, a].reshape(192, 384))
            rh[a, :, pl.ds(pl.multiple_of(dyn * 384, 128), 384)] = hi
            rl[a, :, pl.ds(pl.multiple_of(dyn * 384, 128), 384)] = lo

    def product(j):
        tiles = (rh[...].reshape(768, 768), rl[...].reshape(768, 768))
        got = dot3(tiles, (gh[j].reshape(768, W), gl[j].reshape(768, W)))
        for a in range(4):
            for b in range(4):
                p[j, a + k * (b - a), b + k * (a - b)] = got[192 * a : 192 * a + 192, 128 * b : 128 * b + 128]

    slot_a = [mail.slots(2), mail.slots(2)]
    slot_b = [mail.slots(4), mail.slots(4)]
    slot_d = [mail.slots(3), mail.slots(3)]

    def rs1_start(j):
        am, ap, an = (u + 2) % 4, (u + 1) % 4, (u + 3) % 4
        lo, hi = pl.ds(0, 2), pl.ds(2, 2)
        mail.post(slot_a[j][0], p.at[j, am, lo], ra.at[j, 0], udev(1))
        mail.post(slot_a[j][1], p.at[j, am, hi], ra.at[j, 1], udev(-1))
        mail.post(slot_b[j][0], p.at[j, ap, hi], rb.at[j, 0, hi], udev(1))
        mail.post(slot_b[j][1], p.at[j, an, lo], rb.at[j, 1, lo], udev(-1))

    def rs1_mid(j):
        ap, an = (u + 1) % 4, (u + 3) % 4
        lo, hi = pl.ds(0, 2), pl.ds(2, 2)
        mail.take(slot_a[j][0], ra.at[j, 0], udev(1))
        ra[j, 0] += p[j, ap, 0:2]
        mail.post(slot_b[j][2], ra.at[j, 0], rb.at[j, 0, lo], udev(1))
        mail.take(slot_a[j][1], ra.at[j, 1], udev(-1))
        ra[j, 1] += p[j, an, 2:4]
        mail.post(slot_b[j][3], ra.at[j, 1], rb.at[j, 1, hi], udev(-1))

    def rs1_end(j):
        lo, hi = pl.ds(0, 2), pl.ds(2, 2)
        mail.take(slot_b[j][0], rb.at[j, 0, hi], udev(1))
        mail.take(slot_b[j][1], rb.at[j, 1, lo], udev(-1))
        mail.take(slot_b[j][2], rb.at[j, 0, lo], udev(1))
        mail.take(slot_b[j][3], rb.at[j, 1, hi], udev(-1))
        for d in (2, 1, 3, 0):
            b = (v + d) % 4
            s[j, b] = p[j, u, b] + rb[j, 0, b] + rb[j, 1, b]
            if d:
                mail.post(slot_d[j][d - 1], s.at[j, b], sb.at[j, d - 1], vdev(d))

    slot_i = [mail.slots(3), mail.slots(3)]
    slot_t = mail.slots(2)

    def rs2_end(j):
        for d in range(1, 4):
            mail.take(slot_d[j][d - 1], sb.at[j, d - 1], vdev(d))
        got = s[j, v] + sb[j, 0] + sb[j, 1] + sb[j, 2]
        tx[j, k] = got.reshape(4, 48, 128)
        mail.post(slot_t[j], tx.at[j, k], tx.at[j, k], partner)

    def rows_send(j):
        ib[j, y] = tx[j, k, y]
        for d in range(1, 4):
            mail.post(slot_i[j][d - 1], tx.at[j, k, (y + d) % 4], ib.at[j, y], ydev(d))

    def rows_take(j):
        for d in range(1, 4):
            mail.take(slot_i[j][d - 1], ib.at[j, (y + 4 - d) % 4], ydev(d))
        return jnp.concatenate([ib[j, b] for b in range(4)], axis=1)

    slot_fy = mail.slots(3)
    slot_ftx = mail.slots(1)[0]

    def mates_send():
        mail.take(slot_fx, fy.at[y, other], partner)
        for d in range(1, 4):
            mail.post(slot_fy[d - 1], fy.at[y], fy.at[y], ydev(d))

    def mates_take():
        for d in range(1, 4):
            mail.take(slot_fy[d - 1], fy.at[(y + 4 - d) % 4], ydev(d))
        for c in range(2):
            ft[:, 192 * c : 192 * c + 192] = jnp.concatenate([fy[b, c] for b in range(4)], axis=0).T

    def mates_half():
        copy = mail.desc(slot_ftx, ft.at[pl.ds(0, 256)], ftb, partner)
        pl.when(k == 1)(copy.start)

    def mates_half_take():
        copy = mail.desc(slot_ftx, ft.at[pl.ds(0, 256)], ftb, partner)
        pl.when(k == 0)(copy.wait_recv)
        pl.when(k == 1)(copy.wait_send)

        @pl.when(k == 1)
        def _():
            ftb[...] = ft[256:512]

    slot_x = [mail.slots(3), mail.slots(3)]
    slot_z = [mail.slots(7), mail.slots(7)]
    slot_gz = [mail.slots(7), mail.slots(7)]
    slot_gu = [mail.slots(3), mail.slots(3)]
    slot_gv = [mail.slots(3), mail.slots(3)]
    slot_gc = [mail.slots(4), mail.slots(4)]
    size = (128, 64)

    def cross(j):
        mail.take(slot_t[j], tx.at[j, other], partner)
        tt = halves(jnp.concatenate([tx[j, 0].reshape(192, 128), tx[j, 1].reshape(192, 128)], axis=0))
        left = ft[...] if j == 0 else ftb[...]
        got = dot3(halves(left), tt)
        n = size[j]
        for b in range(4):
            cb[j, b, 0:n] = got[n * b : n * b + n]
        for d in (2, 1, 3):
            mail.post(slot_x[j][d - 1], cb.at[j, (x + d) % 4, pl.ds(0, n)], cx.at[j, d - 1, pl.ds(0, n)], xdev(d))

    def cross_x(j):
        n, e = size[j], size[j] // 8
        total = cb[j, x, 0:n]
        for d in range(1, 4):
            mail.take(slot_x[j][d - 1], cx.at[j, d - 1, pl.ds(0, n)], xdev(d))
            total += cx[j, d - 1, 0:n]
        for b in range(8):
            ct[j, b, 0:e] = total[e * b : e * b + e]
        for d in (4, 3, 5, 2, 6, 1, 7):
            mail.post(slot_z[j][d - 1], ct.at[j, (z + d) % 8, pl.ds(0, e)], cz.at[j, d - 1, pl.ds(0, e)], zdev(d))

    def cross_z(j):
        e = size[j] // 8
        total = ct[j, z, 0:e]
        for d in range(1, 8):
            mail.take(slot_z[j][d - 1], cz.at[j, d - 1, pl.ds(0, e)], zdev(d))
            total += cz[j, d - 1, 0:e]
        piece = cf.at[j, k, v, u, z, pl.ds(0, e)]
        piece[...] = total
        for d in (4, 3, 5, 2, 6, 1, 7):
            mail.post(slot_gz[j][d - 1], piece, piece, zdev(d))

    def cross_u(j):
        e = size[j] // 8
        for d in range(1, 8):
            mail.take(slot_gz[j][d - 1], cf.at[j, k, v, u, (z + 8 - d) % 8, pl.ds(0, e)], zdev(d))
        piece = cf.at[j, k, v, u, :, pl.ds(0, e)]
        for d in (2, 1, 3):
            mail.post(slot_gu[j][d - 1], piece, piece, udev(d))

    def cross_v(j):
        e = size[j] // 8
        for d in range(1, 4):
            mail.take(slot_gu[j][d - 1], cf.at[j, k, v, (u + 4 - d) % 4, :, pl.ds(0, e)], udev(d))
        piece = cf.at[j, k, v, :, :, pl.ds(0, e)]
        for d in (2, 1, 3):
            mail.post(slot_gv[j][d - 1], piece, piece, vdev(d))
        mail.post(slot_gc[j][0], piece, piece, partner)

    def cross_c(j):
        e = size[j] // 8
        for d in (1, 3, 2):
            piece = cf.at[j, k, (v + 4 - d) % 4, :, :, pl.ds(0, e)]
            mail.take(slot_gv[j][d - 1], piece, vdev(d))
            mail.post(slot_gc[j][d], piece, piece, partner)

    def cross_end(j):
        e = size[j] // 8
        for d in range(4):
            mail.take(slot_gc[j][d], cf.at[j, other, (u + 4 - d) % 4, :, :, pl.ds(0, e)], partner)

    def whole(c):
        parts = []
        for b in range(4):
            if c == 0:
                parts.append(cf[0, 0, b].reshape(W, 128))
            else:
                parts.append(cf[0, 1, :, b].reshape(W, 128))
        return jnp.concatenate(parts, axis=1)

    rows_to_column(0)
    tiles_to_partner()
    rows_to_partner()
    for c in load_r:
        c.wait()
    split_r(k)
    rows_to_column(1)
    ring(0, 0)
    ring(1, 0)
    mates_send()
    tiles_take()
    split_r(other)
    ring(0, 1)
    ring(1, 1)
    collect(0, 0)
    collect(1, 0)
    ring(0, 2)
    ring(1, 2)
    collect(0, 1)
    collect(1, 1)
    ring(0, 3)
    ring(1, 3)
    collect(0, 2)
    collect(1, 2)
    ring(0, 4)
    collect(0, 3)
    collect(0, 4)
    product(0)
    rs1_start(0)
    ring(1, 4)
    collect(1, 3)
    collect(1, 4)
    product(1)
    rs1_mid(0)
    rs1_start(1)
    mates_take()
    mates_half()
    load_k.wait()
    kb[0], kb[1] = halves(kk_v[...])
    rs1_end(0)
    rs1_mid(1)
    kb[2], kb[3] = halves(kk_v[...].T)
    rs2_end(0)
    mates_half_take()
    cross(0)
    rows_send(0)
    rs1_end(1)
    cross_x(0)
    rs2_end(1)
    cross(1)
    rows_send(1)
    cross_z(0)
    cross_x(1)
    t_own = rows_take(0)
    o1[...] = -t_own
    out1 = here(o1, inv1_o)
    cross_u(0)
    cross_z(1)
    o2[...] = dot3(halves(t_own), (kb[0], kb[1])) - rows_take(1)
    out2 = here(o2, inv2_o)
    cross_v(0)
    cross_u(1)
    cross_v(1)
    cross_c(0)
    cross_end(0)
    load_d1.wait()
    load_d2.wait()
    ob1[...] = d1_v[...] + whole(0)
    out3 = here(ob1, blk1_o)
    c21 = whole(1)
    oc[...] = c21.T - dot3(halves(ob1[...]), (kb[0], kb[1]))
    out4 = here(oc, cpl_o)
    cross_c(1)
    ob2[...] = d2_v[...] - dot3(halves(c21), (kb[0], kb[1])) - dot3((kb[2], kb[3]), halves(oc[...]))
    cross_end(1)
    for b in range(4):
        for a in range(4):
            cols = slice(128 * b, 128 * b + 128)
            ob2[64 * a : 64 * a + 64, cols] += cf[1, 0, b, a, :, 0:8].reshape(64, 128)
            ob2[256 + 64 * a : 320 + 64 * a, cols] += cf[1, 1, a, b, :, 0:8].reshape(64, 128)
    out5 = here(ob2, blk2_o)
    for copy in mail.sent:
        copy.wait_send()
    for copy in (out1, out2, out3, out4, out5):
        copy.wait()


def place_kernel(*refs):
    held, sem = refs[10:15], refs[15]
    loads = [pltpu.make_async_copy(refs[i], held[i], sem.at[i]) for i in range(5)]
    stores = [pltpu.make_async_copy(held[i], refs[5 + i], sem.at[5 + i]) for i in range(5)]
    for copy in loads:
        copy.start()
    for load, store in zip(loads, stores):
        load.wait()
        store.start()
    for copy in stores:
        copy.wait()


def body(resident, factor_one, pattern_one, factor_two, pattern_two, coupling, diagonal_one, diagonal_two):
    tiles = resident.reshape(4, 4, 2, 48, 384)
    vm = pltpu.VMEM
    any_ = pl.BlockSpec(memory_space=pltpu.HBM)
    sds = jax.ShapeDtypeStruct
    shapes = (sds((48, W), F32), sds((W, W), F32), sds((48, W), F32), sds((W, W), F32), sds((W, W), F32))
    results = pl.pallas_call(
        kernel,
        out_shape=shapes,
        in_specs=[any_] * 8,
        out_specs=(any_,) * 5,
        scratch_shapes=[
            pltpu.SMEM((2, 3), jnp.int32),
            vm((2, 48, W), F32),
            vm((2, 4, 4, 48, 384), F32),
            vm((4, 192, 768), BF),
            vm((4, 192, 768), BF),
            vm((2, 16, 48, W), F32),
            vm((2, 16, 48, W), BF),
            vm((2, 16, 48, W), BF),
            vm((2, 4, 4, 192, 128), F32),
            vm((2, 2, 2, 192, 128), F32),
            vm((2, 2, 4, 192, 128), F32),
            vm((2, 4, 192, 128), F32),
            vm((2, 3, 192, 128), F32),
            vm((2, 4, 48, 128), F32),
            vm((2, 2, 4, 48, 128), F32),
            vm((4, 2, 48, W), F32),
            vm((W, 384), F32),
            vm((256, 384), F32),
            vm((2, 4, 128, 128), F32),
            vm((2, 3, 128, 128), F32),
            vm((2, 8, 16, 128), F32),
            vm((2, 7, 16, 128), F32),
            vm((2, 2, 4, 4, 8, 16, 128), F32),
            vm((W, W), F32),
            vm((4, W, W), BF),
            vm((W, W), F32),
            vm((W, W), F32),
            vm((48, W), F32),
            vm((48, W), F32),
            vm((W, W), F32),
            vm((W, W), F32),
            vm((W, W), F32),
            pltpu.SemaphoreType.DMA((N_MAIL,)),
            pltpu.SemaphoreType.DMA((N_MAIL,)),
            pltpu.SemaphoreType.DMA((N_LOCAL,)),
        ],
        name="selected_inverse",
        compiler_params=pltpu.CompilerParams(
            collective_id=0, has_side_effects=True, vmem_limit_bytes=VMEM_LIMIT
        ),
        cost_estimate=pl.CostEstimate(flops=4_000_000_000, bytes_accessed=8_000_000, transcendentals=0),
    )(tiles, factor_one, pattern_one, factor_two, pattern_two, coupling, diagonal_one, diagonal_two)
    free = pl.BlockSpec(memory_space=pl.ANY)
    return pl.pallas_call(
        place_kernel,
        out_shape=shapes,
        in_specs=[free] * 5,
        out_specs=(free,) * 5,
        scratch_shapes=[vm(shape.shape, F32) for shape in shapes] + [pltpu.SemaphoreType.DMA((10,))],
        name="place_results",
    )(*results)


def solution(mesh):
    return jax.shard_map(
        body,
        mesh=mesh,
        in_specs=(
            P("row", "col"),
            P(("row", "col"), None),
            P(("row", "col")),
            P(("row", "col"), None),
            P(("row", "col")),
            P(),
            P(),
            P(),
        ),
        out_specs=(P(("row", "col"), None), P(), P(("row", "col"), None), P(), P()),
        check_vma=False,
    )
```

```python
import jax
import jax.numpy as jnp
from jax import lax
from jax.experimental import pallas as pl
from jax.experimental.pallas import tpu as pltpu
from jax.sharding import PartitionSpec as P

W = 512
MESH = pl.DeviceIdType.MESH
BF = jnp.bfloat16
F32 = jnp.float32


def halves(value):
    high = value.astype(BF)
    return high, (value - high.astype(F32)).astype(BF)


def dot3(left, right):
    (lh, ll), (rh, rl) = left, right
    total = jnp.dot(lh, rh, preferred_element_type=F32)
    total += jnp.dot(lh, rl, preferred_element_type=F32)
    return total + jnp.dot(ll, rh, preferred_element_type=F32)


class Mail:
    def __init__(self, send, recv):
        self.send, self.recv, self.count, self.sent = send, recv, 0, []

    def slots(self, n):
        first = self.count
        self.count += n
        return list(range(first, first + n))

    def desc(self, slot, src, dst, dev):
        return pltpu.make_async_remote_copy(
            src, dst, self.send.at[slot], self.recv.at[slot], device_id=dev, device_id_type=MESH
        )

    def post(self, slot, src, dst, dev):
        copy = self.desc(slot, src, dst, dev)
        copy.start()
        self.sent.append(copy)

    def take(self, slot, dst, dev):
        self.desc(slot, dst, dst, dev).wait_recv()


N_MAIL = 200
N_LOCAL = 40
VMEM_LIMIT = 60 << 20


def kernel(
    res, fac1, pat1, fac2, pat2, coup, diag1, diag2,
    inv1_o, blk1_o, inv2_o, cpl_o, blk2_o,
    pat, own, rx, rh, rl, g, gh, gl, p, ra, rb, s, sb, ib, tx, fy, ft, ftb, fth, ftl, fbh, fbl,
    cb, cx, ct, cz, cf, kk_v, kb, d1_v, d2_v, o1, o2, ob1, ob2, oc,
    send, recv, local,
):
    z = lax.axis_index("row")
    col = lax.axis_index("col")
    k = col % 2
    x = (col // 2) % 4
    y = col // 8
    other = 1 - k

    def at(xx, yy, zz, kk):
        return (zz, (yy * 4 + xx) * 2 + kk)

    partner = at(x, y, z, other)

    def zdev(d):
        return at(x, y, (z + d + 8) % 8, k)

    def xdev(d):
        return at((x + d + 4) % 4, y, z, k)

    def ydev(d):
        return at(x, (y + d + 4) % 4, z, k)

    u = x + k * (y - x)
    v = y + k * (x - y)

    def udev(d):
        return at((x + (1 - k) * d + 4) % 4, (y + k * d + 4) % 4, z, k)

    def vdev(d):
        return at((x + k * d + 4) % 4, (y + (1 - k) * d + 4) % 4, z, k)

    goal = 2 * z + y // 2
    mine = (y % 2) * 4 + x
    target = at(goal % 4, goal // 4, (mine + 3 * z + 1) % 8, k)
    q = 4 * y + x
    z0 = q // 2
    chunks = {d: (z + d + 63 - 3 * z0) % 8 for d in range(-3, 5)}

    def chunk(d):
        return chunks[(d + 3) % 8 - 3]

    source = at(chunk(0) % 4, 2 * (q % 2) + chunk(0) // 4, z0, k)

    mail = Mail(send, recv)
    used = [0]

    def here(src, dst):
        copy = pltpu.make_async_copy(src, dst, local.at[used[0]])
        used[0] += 1
        copy.start()
        return copy

    load_p = [here(pat1, pat.at[0]), here(pat2, pat.at[1])]
    load_f = [here(fac1, own.at[0]), here(fac2, own.at[1])]
    load_r = [here(res.at[:, a, k], rx.at[k, a]) for a in range(4)]
    load_k = here(coup, kk_v)
    load_d1 = here(diag1, d1_v)
    load_d2 = here(diag2, d2_v)

    barrier = pltpu.get_barrier_semaphore()
    friends = [partner] + [zdev(d) for d in range(1, 8)] + [xdev(d) for d in range(1, 4)] + [ydev(d) for d in range(1, 4)]
    for dev in friends + [source]:
        pl.semaphore_signal(barrier, inc=1, device_id=dev, device_id_type=MESH)

    for j in range(2):
        load_p[j].wait()
        load_f[j].wait()
        for b in range(3):
            own[j, 16 * b : 16 * b + 16] = own[j, 16 * b : 16 * b + 16] * pat[j, b].astype(F32)
    pl.semaphore_wait(barrier, len(friends) + 1)

    slot_perm = mail.slots(2)
    slot_r = mail.slots(4)
    slot_fx = mail.slots(1)[0]

    def rows_to_column(j):
        mail.post(slot_perm[j], own.at[j], g.at[j, 2 * mine + k], target)

    def tiles_to_partner():
        for a in range(4):
            mail.post(slot_r[a], res.at[:, a, other], rx.at[k, a], partner)

    def tiles_take():
        for a in range(4):
            mail.take(slot_r[a], rx.at[other, a], partner)

    def rows_to_partner():
        fy[y, k] = own[k]
        mail.post(slot_fx, own.at[other], fy.at[y, k], partner)

    slot_up = [mail.slots(4), mail.slots(4)]
    slot_dn = [mail.slots(4), mail.slots(4)]
    slot_fwd = [mail.slots(8), mail.slots(8)]

    def split(j, m):
        gh[j, m], gl[j, m] = halves(g[j, m])

    def forward(j, f, d):
        m = 2 * chunk(d) + k
        mail.post(slot_fwd[j][f], g.at[j, m], g.at[j, m], partner)

    def split_own(j, step):
        for d in {0: (0,), 4: (4,)}.get(step, (-step, step)):
            split(j, 2 * chunk(d) + k)

    def arrived(j, f, d):
        m = 2 * chunk(d) + other
        mail.take(slot_fwd[j][f], g.at[j, m], partner)
        split(j, m)

    def ring(j, step):
        m_up = 2 * chunk(-step) + k
        m_dn = 2 * chunk(step) + k
        if step == 0:
            mail.take(slot_perm[j], g.at[j, m_up], target)
            mail.post(slot_up[j][0], g.at[j, m_up], g.at[j, m_up], zdev(1))
            mail.post(slot_dn[j][0], g.at[j, m_up], g.at[j, m_up], zdev(-1))
            return
        lo = g.at[j, m_up]
        hi = g.at[j, m_dn]
        if step == 4:
            mail.take(slot_up[j][3], lo.at[pl.ds(0, 24)], zdev(1))
            mail.take(slot_dn[j][3], hi.at[pl.ds(24, 24)], zdev(-1))
            return
        mail.take(slot_up[j][step - 1], g.at[j, m_up], zdev(1))
        if step == 3:
            mail.post(slot_up[j][3], lo.at[pl.ds(0, 24)], lo.at[pl.ds(0, 24)], zdev(1))
        else:
            mail.post(slot_up[j][step], lo, lo, zdev(1))
        mail.take(slot_dn[j][step - 1], g.at[j, m_dn], zdev(-1))
        if step == 3:
            mail.post(slot_dn[j][3], hi.at[pl.ds(24, 24)], hi.at[pl.ds(24, 24)], zdev(-1))
        else:
            mail.post(slot_dn[j][step], hi, hi, zdev(-1))

    def pass_on(j, step):
        if step in (0, 4):
            forward(j, 0 if step == 0 else 7, step)
        else:
            forward(j, 2 * step - 1, -step)
            forward(j, 2 * step, step)

    def collect(j, step):
        if step in (0, 4):
            arrived(j, 0 if step == 0 else 7, step)
        else:
            arrived(j, 2 * step - 1, -step)
            arrived(j, 2 * step, step)

    def split_r(dyn):
        for a in range(4):
            hi, lo = halves(rx[dyn, a].reshape(192, 384))
            rh[a, :, pl.ds(pl.multiple_of(dyn * 384, 128), 384)] = hi
            rl[a, :, pl.ds(pl.multiple_of(dyn * 384, 128), 384)] = lo

    def product(j):
        tiles = (rh[...].reshape(768, 768), rl[...].reshape(768, 768))
        got = dot3(tiles, (gh[j].reshape(768, W), gl[j].reshape(768, W)))
        for a in range(4):
            for b in range(4):
                p[j, a + k * (b - a), b + k * (a - b)] = got[192 * a : 192 * a + 192, 128 * b : 128 * b + 128]

    slot_a = [mail.slots(2), mail.slots(2)]
    slot_b = [mail.slots(4), mail.slots(4)]
    slot_d = [mail.slots(3), mail.slots(3)]

    def rs1_start(j):
        am, ap, an = (u + 2) % 4, (u + 1) % 4, (u + 3) % 4
        lo, hi = pl.ds(0, 2), pl.ds(2, 2)
        mail.post(slot_a[j][0], p.at[j, am, lo], ra.at[j, 0], udev(1))
        mail.post(slot_a[j][1], p.at[j, am, hi], ra.at[j, 1], udev(-1))
        mail.post(slot_b[j][0], p.at[j, ap, hi], rb.at[j, 0, hi], udev(1))
        mail.post(slot_b[j][1], p.at[j, an, lo], rb.at[j, 1, lo], udev(-1))

    def rs1_mid(j):
        ap, an = (u + 1) % 4, (u + 3) % 4
        lo, hi = pl.ds(0, 2), pl.ds(2, 2)
        mail.take(slot_a[j][0], ra.at[j, 0], udev(1))
        ra[j, 0] += p[j, ap, 0:2]
        mail.post(slot_b[j][2], ra.at[j, 0], rb.at[j, 0, lo], udev(1))
        mail.take(slot_a[j][1], ra.at[j, 1], udev(-1))
        ra[j, 1] += p[j, an, 2:4]
        mail.post(slot_b[j][3], ra.at[j, 1], rb.at[j, 1, hi], udev(-1))

    def rs1_end(j):
        lo, hi = pl.ds(0, 2), pl.ds(2, 2)
        mail.take(slot_b[j][0], rb.at[j, 0, hi], udev(1))
        mail.take(slot_b[j][1], rb.at[j, 1, lo], udev(-1))
        mail.take(slot_b[j][2], rb.at[j, 0, lo], udev(1))
        mail.take(slot_b[j][3], rb.at[j, 1, hi], udev(-1))
        for d in (2, 1, 3, 0):
            b = (v + d) % 4
            s[j, b] = p[j, u, b] + rb[j, 0, b] + rb[j, 1, b]
            if d:
                mail.post(slot_d[j][d - 1], s.at[j, b], sb.at[j, d - 1], vdev(d))

    slot_i = [mail.slots(3), mail.slots(3)]
    slot_t = mail.slots(2)

    def rs2_end(j):
        for d in range(1, 4):
            mail.take(slot_d[j][d - 1], sb.at[j, d - 1], vdev(d))
        got = s[j, v] + sb[j, 0] + sb[j, 1] + sb[j, 2]
        tx[j, k] = got.reshape(4, 48, 128)
        mail.post(slot_t[j], tx.at[j, k], tx.at[j, k], partner)

    def rows_send(j):
        ib[j, y] = tx[j, k, y]
        for d in range(1, 4):
            mail.post(slot_i[j][d - 1], tx.at[j, k, (y + d) % 4], ib.at[j, y], ydev(d))

    def rows_take(j):
        for d in range(1, 4):
            mail.take(slot_i[j][d - 1], ib.at[j, (y + 4 - d) % 4], ydev(d))
        return jnp.concatenate([ib[j, b] for b in range(4)], axis=1)

    slot_fy = mail.slots(3)
    slot_ftx = mail.slots(1)[0]

    def mates_send():
        mail.take(slot_fx, fy.at[y, other], partner)
        for d in range(1, 4):
            mail.post(slot_fy[d - 1], fy.at[y], fy.at[y], ydev(d))

    def mates_take():
        for d in range(1, 4):
            mail.take(slot_fy[d - 1], fy.at[(y + 4 - d) % 4], ydev(d))
        for c in range(2):
            ft[:, 192 * c : 192 * c + 192] = jnp.concatenate([fy[b, c] for b in range(4)], axis=0).T
        fth[...], ftl[...] = halves(ft[...])

    def mates_half():
        copy = mail.desc(slot_ftx, ft.at[pl.ds(0, 256)], ftb, partner)
        pl.when(k == 1)(copy.start)

    def mates_half_take():
        copy = mail.desc(slot_ftx, ft.at[pl.ds(0, 256)], ftb, partner)
        pl.when(k == 0)(copy.wait_recv)
        pl.when(k == 1)(copy.wait_send)

        @pl.when(k == 1)
        def _():
            ftb[...] = ft[256:512]

        fbh[...], fbl[...] = halves(ftb[...])

    slot_x = [mail.slots(3), mail.slots(3)]
    slot_z = [mail.slots(7), mail.slots(7)]
    slot_gz = [mail.slots(7), mail.slots(7)]
    slot_gu = [mail.slots(3), mail.slots(3)]
    slot_gv = [mail.slots(3), mail.slots(3)]
    slot_gc = [mail.slots(4), mail.slots(4)]
    size = (128, 64)

    def cross(j):
        mail.take(slot_t[j], tx.at[j, other], partner)
        tt = halves(jnp.concatenate([tx[j, 0].reshape(192, 128), tx[j, 1].reshape(192, 128)], axis=0))
        left = (fth[...], ftl[...]) if j == 0 else (fbh[...], fbl[...])
        got = dot3(left, tt)
        n = size[j]
        for b in range(4):
            cb[j, b, 0:n] = got[n * b : n * b + n]
        for d in (2, 1, 3):
            mail.post(slot_x[j][d - 1], cb.at[j, (x + d) % 4, pl.ds(0, n)], cx.at[j, d - 1, pl.ds(0, n)], xdev(d))

    def cross_x(j):
        n, e = size[j], size[j] // 8
        total = cb[j, x, 0:n]
        for d in range(1, 4):
            mail.take(slot_x[j][d - 1], cx.at[j, d - 1, pl.ds(0, n)], xdev(d))
            total += cx[j, d - 1, 0:n]
        for b in range(8):
            ct[j, b, 0:e] = total[e * b : e * b + e]
        for d in (4, 3, 5, 2, 6, 1, 7):
            mail.post(slot_z[j][d - 1], ct.at[j, (z + d) % 8, pl.ds(0, e)], cz.at[j, d - 1, pl.ds(0, e)], zdev(d))

    def cross_z(j):
        e = size[j] // 8
        total = ct[j, z, 0:e]
        for d in range(1, 8):
            mail.take(slot_z[j][d - 1], cz.at[j, d - 1, pl.ds(0, e)], zdev(d))
            total += cz[j, d - 1, 0:e]
        piece = cf.at[j, k, v, u, z, pl.ds(0, e)]
        piece[...] = total
        for d in (4, 3, 5, 2, 6, 1, 7):
            mail.post(slot_gz[j][d - 1], piece, piece, zdev(d))

    def cross_u(j):
        e = size[j] // 8
        for d in range(1, 8):
            mail.take(slot_gz[j][d - 1], cf.at[j, k, v, u, (z + 8 - d) % 8, pl.ds(0, e)], zdev(d))
        piece = cf.at[j, k, v, u, :, pl.ds(0, e)]
        for d in (2, 1, 3):
            mail.post(slot_gu[j][d - 1], piece, piece, udev(d))

    def cross_v(j):
        e = size[j] // 8
        for d in range(1, 4):
            mail.take(slot_gu[j][d - 1], cf.at[j, k, v, (u + 4 - d) % 4, :, pl.ds(0, e)], udev(d))
        piece = cf.at[j, k, v, :, :, pl.ds(0, e)]
        for d in (2, 1, 3):
            mail.post(slot_gv[j][d - 1], piece, piece, vdev(d))
        mail.post(slot_gc[j][0], piece, piece, partner)

    def cross_c(j):
        e = size[j] // 8
        for d in (1, 3, 2):
            piece = cf.at[j, k, (v + 4 - d) % 4, :, :, pl.ds(0, e)]
            mail.take(slot_gv[j][d - 1], piece, vdev(d))
            mail.post(slot_gc[j][d], piece, piece, partner)

    def cross_end(j):
        e = size[j] // 8
        for d in range(4):
            mail.take(slot_gc[j][d], cf.at[j, other, (u + 4 - d) % 4, :, :, pl.ds(0, e)], partner)

    def whole(c):
        parts = []
        for b in range(4):
            if c == 0:
                parts.append(cf[0, 0, b].reshape(W, 128))
            else:
                parts.append(cf[0, 1, :, b].reshape(W, 128))
        return jnp.concatenate(parts, axis=1)

    rows_to_column(0)
    tiles_to_partner()
    rows_to_partner()
    for c in load_r:
        c.wait()
    split_r(k)
    rows_to_column(1)
    ring(0, 0)
    pass_on(0, 0)
    ring(1, 0)
    pass_on(1, 0)
    mates_send()
    split_own(0, 0)
    split_own(1, 0)
    tiles_take()
    split_r(other)
    for step in (1, 2, 3):
        ring(0, step)
        ring(1, step)
        pass_on(0, step)
        pass_on(1, step)
        split_own(0, step)
        split_own(1, step)
        collect(0, step - 1)
        collect(1, step - 1)
    ring(0, 4)
    pass_on(0, 4)
    split_own(0, 4)
    collect(0, 3)
    collect(0, 4)
    product(0)
    rs1_start(0)
    ring(1, 4)
    pass_on(1, 4)
    split_own(1, 4)
    collect(1, 3)
    collect(1, 4)
    product(1)
    rs1_mid(0)
    rs1_start(1)
    mates_take()
    mates_half()
    load_k.wait()
    kb[0], kb[1] = halves(kk_v[...])
    rs1_end(0)
    rs1_mid(1)
    kb[2], kb[3] = halves(kk_v[...].T)
    rs2_end(0)
    mates_half_take()
    cross(0)
    rows_send(0)
    rs1_end(1)
    cross_x(0)
    rs2_end(1)
    cross(1)
    rows_send(1)
    cross_z(0)
    cross_x(1)
    t_own = rows_take(0)
    o1[...] = -t_own
    out1 = here(o1, inv1_o)
    cross_u(0)
    cross_z(1)
    o2[...] = dot3(halves(t_own), (kb[0], kb[1])) - rows_take(1)
    out2 = here(o2, inv2_o)
    cross_v(0)
    cross_u(1)
    cross_v(1)
    cross_c(0)
    cross_end(0)
    load_d1.wait()
    load_d2.wait()
    ob1[...] = d1_v[...] + whole(0)
    out3 = here(ob1, blk1_o)
    c21 = whole(1)
    oc[...] = c21.T - dot3(halves(ob1[...]), (kb[0], kb[1]))
    out4 = here(oc, cpl_o)
    cross_c(1)
    ob2[...] = d2_v[...] - dot3(halves(c21), (kb[0], kb[1])) - dot3((kb[2], kb[3]), halves(oc[...]))
    cross_end(1)
    for b in range(4):
        for a in range(4):
            cols = slice(128 * b, 128 * b + 128)
            ob2[64 * a : 64 * a + 64, cols] += cf[1, 0, b, a, :, 0:8].reshape(64, 128)
            ob2[256 + 64 * a : 320 + 64 * a, cols] += cf[1, 1, a, b, :, 0:8].reshape(64, 128)
    out5 = here(ob2, blk2_o)
    for copy in mail.sent:
        copy.wait_send()
    for copy in (out1, out2, out3, out4, out5):
        copy.wait()


def place_kernel(*refs):
    held, sem = refs[10:15], refs[15]
    loads = [pltpu.make_async_copy(refs[i], held[i], sem.at[i]) for i in range(5)]
    stores = [pltpu.make_async_copy(held[i], refs[5 + i], sem.at[5 + i]) for i in range(5)]
    for copy in loads:
        copy.start()
    for load, store in zip(loads, stores):
        load.wait()
        store.start()
    for copy in stores:
        copy.wait()


def body(resident, factor_one, pattern_one, factor_two, pattern_two, coupling, diagonal_one, diagonal_two):
    tiles = resident.reshape(4, 4, 2, 48, 384)
    vm = pltpu.VMEM
    any_ = pl.BlockSpec(memory_space=pltpu.HBM)
    sds = jax.ShapeDtypeStruct
    shapes = (sds((48, W), F32), sds((W, W), F32), sds((48, W), F32), sds((W, W), F32), sds((W, W), F32))
    results = pl.pallas_call(
        kernel,
        out_shape=shapes,
        in_specs=[any_] * 8,
        out_specs=(any_,) * 5,
        scratch_shapes=[
            pltpu.SMEM((2, 3), jnp.int32),
            vm((2, 48, W), F32),
            vm((2, 4, 4, 48, 384), F32),
            vm((4, 192, 768), BF),
            vm((4, 192, 768), BF),
            vm((2, 16, 48, W), F32),
            vm((2, 16, 48, W), BF),
            vm((2, 16, 48, W), BF),
            vm((2, 4, 4, 192, 128), F32),
            vm((2, 2, 2, 192, 128), F32),
            vm((2, 2, 4, 192, 128), F32),
            vm((2, 4, 192, 128), F32),
            vm((2, 3, 192, 128), F32),
            vm((2, 4, 48, 128), F32),
            vm((2, 2, 4, 48, 128), F32),
            vm((4, 2, 48, W), F32),
            vm((W, 384), F32),
            vm((256, 384), F32),
            vm((W, 384), BF),
            vm((W, 384), BF),
            vm((256, 384), BF),
            vm((256, 384), BF),
            vm((2, 4, 128, 128), F32),
            vm((2, 3, 128, 128), F32),
            vm((2, 8, 16, 128), F32),
            vm((2, 7, 16, 128), F32),
            vm((2, 2, 4, 4, 8, 16, 128), F32),
            vm((W, W), F32),
            vm((4, W, W), BF),
            vm((W, W), F32),
            vm((W, W), F32),
            vm((48, W), F32),
            vm((48, W), F32),
            vm((W, W), F32),
            vm((W, W), F32),
            vm((W, W), F32),
            pltpu.SemaphoreType.DMA((N_MAIL,)),
            pltpu.SemaphoreType.DMA((N_MAIL,)),
            pltpu.SemaphoreType.DMA((N_LOCAL,)),
        ],
        name="selected_inverse",
        compiler_params=pltpu.CompilerParams(
            collective_id=0, has_side_effects=True, vmem_limit_bytes=VMEM_LIMIT
        ),
        cost_estimate=pl.CostEstimate(flops=4_000_000_000, bytes_accessed=8_000_000, transcendentals=0),
    )(tiles, factor_one, pattern_one, factor_two, pattern_two, coupling, diagonal_one, diagonal_two)
    free = pl.BlockSpec(memory_space=pl.ANY)
    return pl.pallas_call(
        place_kernel,
        out_shape=shapes,
        in_specs=[free] * 5,
        out_specs=(free,) * 5,
        scratch_shapes=[vm(shape.shape, F32) for shape in shapes] + [pltpu.SemaphoreType.DMA((10,))],
        name="place_results",
    )(*results)


def solution(mesh):
    return jax.shard_map(
        body,
        mesh=mesh,
        in_specs=(
            P("row", "col"),
            P(("row", "col"), None),
            P(("row", "col")),
            P(("row", "col"), None),
            P(("row", "col")),
            P(),
            P(),
            P(),
        ),
        out_specs=(P(("row", "col"), None), P(), P(("row", "col"), None), P(), P()),
        check_vma=False,
    )
```

```python
import jax
import jax.numpy as jnp
from jax import lax
from jax.experimental import pallas as pl
from jax.experimental.pallas import tpu as pltpu
from jax.sharding import PartitionSpec as P

W = 512
MESH = pl.DeviceIdType.MESH
BF = jnp.bfloat16
F32 = jnp.float32


def halves(value):
    high = value.astype(BF)
    return high, (value - high.astype(F32)).astype(BF)


def dot3(left, right):
    (lh, ll), (rh, rl) = left, right
    total = jnp.dot(lh, rh, preferred_element_type=F32)
    total += jnp.dot(lh, rl, preferred_element_type=F32)
    return total + jnp.dot(ll, rh, preferred_element_type=F32)


class Mail:
    def __init__(self, send, recv):
        self.send, self.recv, self.count, self.sent = send, recv, 0, []

    def slots(self, n):
        first = self.count
        self.count += n
        return list(range(first, first + n))

    def desc(self, slot, src, dst, dev):
        return pltpu.make_async_remote_copy(
            src, dst, self.send.at[slot], self.recv.at[slot], device_id=dev, device_id_type=MESH
        )

    def post(self, slot, src, dst, dev):
        copy = self.desc(slot, src, dst, dev)
        copy.start()
        self.sent.append(copy)

    def take(self, slot, dst, dev):
        self.desc(slot, dst, dst, dev).wait_recv()


N_MAIL = 200
N_LOCAL = 40
VMEM_LIMIT = 60 << 20


def kernel(
    res, fac1, pat1, fac2, pat2, coup, diag1, diag2,
    inv1_o, blk1_o, inv2_o, cpl_o, blk2_o,
    pat, own, rx, rh, rl, g, gh, gl, p, ra, rb, s, sb, ib, tx, fy, ft, ftb, fth, ftl, fbh, fbl,
    cb, cx, ct, cz, cf, kk_v, kb, d1_v, d2_v, o1, o2, ob1, ob2, oc,
    send, recv, local,
):
    z = lax.axis_index("row")
    col = lax.axis_index("col")
    k = col % 2
    x = (col // 2) % 4
    y = col // 8
    other = 1 - k

    def at(xx, yy, zz, kk):
        return (zz, (yy * 4 + xx) * 2 + kk)

    partner = at(x, y, z, other)

    def zdev(d):
        return at(x, y, (z + d + 8) % 8, k)

    def xdev(d):
        return at((x + d + 4) % 4, y, z, k)

    def ydev(d):
        return at(x, (y + d + 4) % 4, z, k)

    u = x + k * (y - x)
    v = y + k * (x - y)

    def udev(d):
        return at((x + (1 - k) * d + 4) % 4, (y + k * d + 4) % 4, z, k)

    def vdev(d):
        return at((x + k * d + 4) % 4, (y + (1 - k) * d + 4) % 4, z, k)

    goal = 2 * z + y // 2
    mine = (y % 2) * 4 + x
    targets = [at(goal % 4, goal // 4, (mine + 3 * z + far + 1) % 8, k) for far in (0, 4)]
    q = 4 * y + x
    z0 = q // 2
    chunks = {d: (z + d + 63 - 3 * z0) % 8 for d in range(-3, 5)}

    def chunk(d):
        return chunks[(d + 3) % 8 - 3]

    sources = [at(chunk(d) % 4, 2 * (q % 2) + chunk(d) // 4, z0, k) for d in (0, 4)]

    mail = Mail(send, recv)
    used = [0]

    def here(src, dst):
        copy = pltpu.make_async_copy(src, dst, local.at[used[0]])
        used[0] += 1
        copy.start()
        return copy

    load_p = [here(pat1, pat.at[0]), here(pat2, pat.at[1])]
    load_f = [here(fac1, own.at[0]), here(fac2, own.at[1])]
    load_r = [here(res.at[:, a, k], rx.at[k, a]) for a in range(4)]
    load_k = here(coup, kk_v)
    load_d1 = here(diag1, d1_v)
    load_d2 = here(diag2, d2_v)

    barrier = pltpu.get_barrier_semaphore()
    friends = [partner] + [zdev(d) for d in range(1, 8)] + [xdev(d) for d in range(1, 4)] + [ydev(d) for d in range(1, 4)]
    for dev in friends + sources:
        pl.semaphore_signal(barrier, inc=1, device_id=dev, device_id_type=MESH)

    for j in range(2):
        load_p[j].wait()
        load_f[j].wait()
        for b in range(3):
            own[j, 16 * b : 16 * b + 16] = own[j, 16 * b : 16 * b + 16] * pat[j, b].astype(F32)
    pl.semaphore_wait(barrier, len(friends) + 2)

    slot_perm = [mail.slots(2), mail.slots(2)]
    slot_r = mail.slots(4)
    slot_fx = mail.slots(1)[0]

    def rows_to_column(j):
        for n in range(2):
            mail.post(slot_perm[j][n], own.at[j], g.at[j, 2 * mine + k], targets[n])

    def tiles_to_partner():
        for a in range(4):
            mail.post(slot_r[a], res.at[:, a, other], rx.at[k, a], partner)

    def tiles_take():
        for a in range(4):
            mail.take(slot_r[a], rx.at[other, a], partner)

    def rows_to_partner():
        fy[y, k] = own[k]
        mail.post(slot_fx, own.at[other], fy.at[y, k], partner)

    slot_up = [mail.slots(3), mail.slots(3)]
    slot_dn = [mail.slots(3), mail.slots(3)]
    slot_fwd = [mail.slots(8), mail.slots(8)]

    def split(j, m):
        gh[j, m], gl[j, m] = halves(g[j, m])

    def forward(j, f, d):
        m = 2 * chunk(d) + k
        mail.post(slot_fwd[j][f], g.at[j, m], g.at[j, m], partner)

    def split_own(j, step):
        for d in {0: (0,), 4: (4,)}.get(step, (-step, step)):
            split(j, 2 * chunk(d) + k)

    def arrived(j, f, d):
        m = 2 * chunk(d) + other
        mail.take(slot_fwd[j][f], g.at[j, m], partner)
        split(j, m)

    gets = [(0, 4), (-1, 1, 3, -3), (-2, 2)]
    place_of = {d: f for f, d in enumerate(sum(gets, ()))}

    def ring(j, step):
        def ref(d):
            return g.at[j, 2 * chunk(d) + k]

        if step == 0:
            for n, d in enumerate((0, 4)):
                mail.take(slot_perm[j][n], ref(d), targets[n])
                mail.post(slot_up[j][n], ref(d), ref(d), zdev(1))
                mail.post(slot_dn[j][n], ref(d), ref(d), zdev(-1))
        elif step == 1:
            mail.take(slot_up[j][0], ref(-1), zdev(1))
            mail.post(slot_up[j][2], ref(-1), ref(-1), zdev(1))
            mail.take(slot_dn[j][0], ref(1), zdev(-1))
            mail.post(slot_dn[j][2], ref(1), ref(1), zdev(-1))
            mail.take(slot_up[j][1], ref(3), zdev(1))
            mail.take(slot_dn[j][1], ref(-3), zdev(-1))
        else:
            mail.take(slot_up[j][2], ref(-2), zdev(1))
            mail.take(slot_dn[j][2], ref(2), zdev(-1))

    def pass_on(j, step):
        for d in gets[step]:
            forward(j, place_of[d], d)

    def split_own(j, step):
        for d in gets[step]:
            split(j, 2 * chunk(d) + k)

    def collect(j, step):
        for d in gets[step]:
            arrived(j, place_of[d], d)

    def split_r(dyn):
        for a in range(4):
            hi, lo = halves(rx[dyn, a].reshape(192, 384))
            rh[a, :, pl.ds(pl.multiple_of(dyn * 384, 128), 384)] = hi
            rl[a, :, pl.ds(pl.multiple_of(dyn * 384, 128), 384)] = lo

    def product(j):
        tiles = (rh[...].reshape(768, 768), rl[...].reshape(768, 768))
        got = dot3(tiles, (gh[j].reshape(768, W), gl[j].reshape(768, W)))
        for a in range(4):
            for b in range(4):
                p[j, a + k * (b - a), b + k * (a - b)] = got[192 * a : 192 * a + 192, 128 * b : 128 * b + 128]

    slot_a = [mail.slots(2), mail.slots(2)]
    slot_b = [mail.slots(4), mail.slots(4)]
    slot_d = [mail.slots(3), mail.slots(3)]

    def rs1_start(j):
        am, ap, an = (u + 2) % 4, (u + 1) % 4, (u + 3) % 4
        lo, hi = pl.ds(0, 2), pl.ds(2, 2)
        mail.post(slot_a[j][0], p.at[j, am, lo], ra.at[j, 0], udev(1))
        mail.post(slot_a[j][1], p.at[j, am, hi], ra.at[j, 1], udev(-1))
        mail.post(slot_b[j][0], p.at[j, ap, hi], rb.at[j, 0, hi], udev(1))
        mail.post(slot_b[j][1], p.at[j, an, lo], rb.at[j, 1, lo], udev(-1))

    def rs1_mid(j):
        ap, an = (u + 1) % 4, (u + 3) % 4
        lo, hi = pl.ds(0, 2), pl.ds(2, 2)
        mail.take(slot_a[j][0], ra.at[j, 0], udev(1))
        ra[j, 0] += p[j, ap, 0:2]
        mail.post(slot_b[j][2], ra.at[j, 0], rb.at[j, 0, lo], udev(1))
        mail.take(slot_a[j][1], ra.at[j, 1], udev(-1))
        ra[j, 1] += p[j, an, 2:4]
        mail.post(slot_b[j][3], ra.at[j, 1], rb.at[j, 1, hi], udev(-1))

    def rs1_end(j):
        lo, hi = pl.ds(0, 2), pl.ds(2, 2)
        mail.take(slot_b[j][0], rb.at[j, 0, hi], udev(1))
        mail.take(slot_b[j][1], rb.at[j, 1, lo], udev(-1))
        mail.take(slot_b[j][2], rb.at[j, 0, lo], udev(1))
        mail.take(slot_b[j][3], rb.at[j, 1, hi], udev(-1))
        for d in (2, 1, 3, 0):
            b = (v + d) % 4
            s[j, b] = p[j, u, b] + rb[j, 0, b] + rb[j, 1, b]
            if d:
                mail.post(slot_d[j][d - 1], s.at[j, b], sb.at[j, d - 1], vdev(d))

    slot_i = [mail.slots(3), mail.slots(3)]
    slot_t = mail.slots(2)

    def rs2_end(j):
        for d in range(1, 4):
            mail.take(slot_d[j][d - 1], sb.at[j, d - 1], vdev(d))
        got = s[j, v] + sb[j, 0] + sb[j, 1] + sb[j, 2]
        tx[j, k] = got.reshape(4, 48, 128)
        mail.post(slot_t[j], tx.at[j, k], tx.at[j, k], partner)

    def rows_send(j):
        ib[j, y] = tx[j, k, y]
        for d in range(1, 4):
            mail.post(slot_i[j][d - 1], tx.at[j, k, (y + d) % 4], ib.at[j, y], ydev(d))

    def rows_take(j):
        for d in range(1, 4):
            mail.take(slot_i[j][d - 1], ib.at[j, (y + 4 - d) % 4], ydev(d))
        return jnp.concatenate([ib[j, b] for b in range(4)], axis=1)

    slot_fy = mail.slots(3)
    slot_ftx = mail.slots(1)[0]

    def mates_send():
        mail.take(slot_fx, fy.at[y, other], partner)
        for d in range(1, 4):
            mail.post(slot_fy[d - 1], fy.at[y], fy.at[y], ydev(d))

    def mates_take():
        for d in range(1, 4):
            mail.take(slot_fy[d - 1], fy.at[(y + 4 - d) % 4], ydev(d))
        for c in range(2):
            ft[:, 192 * c : 192 * c + 192] = jnp.concatenate([fy[b, c] for b in range(4)], axis=0).T
        fth[...], ftl[...] = halves(ft[...])

    def mates_half():
        copy = mail.desc(slot_ftx, ft.at[pl.ds(0, 256)], ftb, partner)
        pl.when(k == 1)(copy.start)

    def mates_half_take():
        copy = mail.desc(slot_ftx, ft.at[pl.ds(0, 256)], ftb, partner)
        pl.when(k == 0)(copy.wait_recv)
        pl.when(k == 1)(copy.wait_send)

        @pl.when(k == 1)
        def _():
            ftb[...] = ft[256:512]

        fbh[...], fbl[...] = halves(ftb[...])

    slot_x = [mail.slots(3), mail.slots(3)]
    slot_z = [mail.slots(7), mail.slots(7)]
    slot_gz = [mail.slots(7), mail.slots(7)]
    slot_gu = [mail.slots(3), mail.slots(3)]
    slot_gv = [mail.slots(3), mail.slots(3)]
    slot_gc = [mail.slots(4), mail.slots(4)]
    size = (128, 64)

    def cross(j):
        mail.take(slot_t[j], tx.at[j, other], partner)
        tt = halves(jnp.concatenate([tx[j, 0].reshape(192, 128), tx[j, 1].reshape(192, 128)], axis=0))
        left = (fth[...], ftl[...]) if j == 0 else (fbh[...], fbl[...])
        got = dot3(left, tt)
        n = size[j]
        for b in range(4):
            cb[j, b, 0:n] = got[n * b : n * b + n]
        for d in (2, 1, 3):
            mail.post(slot_x[j][d - 1], cb.at[j, (x + d) % 4, pl.ds(0, n)], cx.at[j, d - 1, pl.ds(0, n)], xdev(d))

    def cross_x(j):
        n, e = size[j], size[j] // 8
        total = cb[j, x, 0:n]
        for d in range(1, 4):
            mail.take(slot_x[j][d - 1], cx.at[j, d - 1, pl.ds(0, n)], xdev(d))
            total += cx[j, d - 1, 0:n]
        for b in range(8):
            ct[j, b, 0:e] = total[e * b : e * b + e]
        for d in (4, 3, 5, 2, 6, 1, 7):
            mail.post(slot_z[j][d - 1], ct.at[j, (z + d) % 8, pl.ds(0, e)], cz.at[j, d - 1, pl.ds(0, e)], zdev(d))

    def cross_z(j):
        e = size[j] // 8
        total = ct[j, z, 0:e]
        for d in range(1, 8):
            mail.take(slot_z[j][d - 1], cz.at[j, d - 1, pl.ds(0, e)], zdev(d))
            total += cz[j, d - 1, 0:e]
        piece = cf.at[j, k, v, u, z, pl.ds(0, e)]
        piece[...] = total
        for d in (4, 3, 5, 2, 6, 1, 7):
            mail.post(slot_gz[j][d - 1], piece, piece, zdev(d))

    def cross_u(j):
        e = size[j] // 8
        for d in range(1, 8):
            mail.take(slot_gz[j][d - 1], cf.at[j, k, v, u, (z + 8 - d) % 8, pl.ds(0, e)], zdev(d))
        piece = cf.at[j, k, v, u, :, pl.ds(0, e)]
        for d in (2, 1, 3):
            mail.post(slot_gu[j][d - 1], piece, piece, udev(d))

    def cross_v(j):
        e = size[j] // 8
        for d in range(1, 4):
            mail.take(slot_gu[j][d - 1], cf.at[j, k, v, (u + 4 - d) % 4, :, pl.ds(0, e)], udev(d))
        piece = cf.at[j, k, v, :, :, pl.ds(0, e)]
        for d in (2, 1, 3):
            mail.post(slot_gv[j][d - 1], piece, piece, vdev(d))
        mail.post(slot_gc[j][0], piece, piece, partner)

    def cross_c(j):
        e = size[j] // 8
        for d in (1, 3, 2):
            piece = cf.at[j, k, (v + 4 - d) % 4, :, :, pl.ds(0, e)]
            mail.take(slot_gv[j][d - 1], piece, vdev(d))
            mail.post(slot_gc[j][d], piece, piece, partner)

    def cross_end(j):
        e = size[j] // 8
        for d in range(4):
            mail.take(slot_gc[j][d], cf.at[j, other, (u + 4 - d) % 4, :, :, pl.ds(0, e)], partner)

    def whole(c):
        parts = []
        for b in range(4):
            if c == 0:
                parts.append(cf[0, 0, b].reshape(W, 128))
            else:
                parts.append(cf[0, 1, :, b].reshape(W, 128))
        return jnp.concatenate(parts, axis=1)

    rows_to_column(0)
    tiles_to_partner()
    rows_to_partner()
    for c in load_r:
        c.wait()
    split_r(k)
    rows_to_column(1)
    ring(0, 0)
    pass_on(0, 0)
    ring(1, 0)
    pass_on(1, 0)
    mates_send()
    split_own(0, 0)
    split_own(1, 0)
    tiles_take()
    split_r(other)
    ring(0, 1)
    pass_on(0, 1)
    collect(0, 0)
    split_own(0, 1)
    ring(1, 1)
    pass_on(1, 1)
    collect(1, 0)
    split_own(1, 1)
    ring(0, 2)
    pass_on(0, 2)
    split_own(0, 2)
    collect(0, 1)
    collect(0, 2)
    product(0)
    rs1_start(0)
    ring(1, 2)
    pass_on(1, 2)
    split_own(1, 2)
    collect(1, 1)
    collect(1, 2)
    product(1)
    rs1_mid(0)
    rs1_start(1)
    mates_take()
    mates_half()
    load_k.wait()
    kb[0], kb[1] = halves(kk_v[...])
    rs1_end(0)
    rs1_mid(1)
    kb[2], kb[3] = halves(kk_v[...].T)
    rs2_end(0)
    mates_half_take()
    cross(0)
    rows_send(0)
    rs1_end(1)
    cross_x(0)
    rs2_end(1)
    cross(1)
    rows_send(1)
    cross_z(0)
    cross_x(1)
    t_own = rows_take(0)
    o1[...] = -t_own
    out1 = here(o1, inv1_o)
    cross_u(0)
    cross_z(1)
    o2[...] = dot3(halves(t_own), (kb[0], kb[1])) - rows_take(1)
    out2 = here(o2, inv2_o)
    cross_v(0)
    cross_u(1)
    cross_v(1)
    cross_c(0)
    cross_end(0)
    load_d1.wait()
    load_d2.wait()
    ob1[...] = d1_v[...] + whole(0)
    out3 = here(ob1, blk1_o)
    c21 = whole(1)
    oc[...] = c21.T - dot3(halves(ob1[...]), (kb[0], kb[1]))
    out4 = here(oc, cpl_o)
    cross_c(1)
    ob2[...] = d2_v[...] - dot3(halves(c21), (kb[0], kb[1])) - dot3((kb[2], kb[3]), halves(oc[...]))
    cross_end(1)
    for b in range(4):
        for a in range(4):
            cols = slice(128 * b, 128 * b + 128)
            ob2[64 * a : 64 * a + 64, cols] += cf[1, 0, b, a, :, 0:8].reshape(64, 128)
            ob2[256 + 64 * a : 320 + 64 * a, cols] += cf[1, 1, a, b, :, 0:8].reshape(64, 128)
    out5 = here(ob2, blk2_o)
    for copy in mail.sent:
        copy.wait_send()
    for copy in (out1, out2, out3, out4, out5):
        copy.wait()


def place_kernel(*refs):
    held, sem = refs[10:15], refs[15]
    loads = [pltpu.make_async_copy(refs[i], held[i], sem.at[i]) for i in range(5)]
    stores = [pltpu.make_async_copy(held[i], refs[5 + i], sem.at[5 + i]) for i in range(5)]
    for copy in loads:
        copy.start()
    for load, store in zip(loads, stores):
        load.wait()
        store.start()
    for copy in stores:
        copy.wait()


def body(resident, factor_one, pattern_one, factor_two, pattern_two, coupling, diagonal_one, diagonal_two):
    tiles = resident.reshape(4, 4, 2, 48, 384)
    vm = pltpu.VMEM
    any_ = pl.BlockSpec(memory_space=pltpu.HBM)
    sds = jax.ShapeDtypeStruct
    shapes = (sds((48, W), F32), sds((W, W), F32), sds((48, W), F32), sds((W, W), F32), sds((W, W), F32))
    results = pl.pallas_call(
        kernel,
        out_shape=shapes,
        in_specs=[any_] * 8,
        out_specs=(any_,) * 5,
        scratch_shapes=[
            pltpu.SMEM((2, 3), jnp.int32),
            vm((2, 48, W), F32),
            vm((2, 4, 4, 48, 384), F32),
            vm((4, 192, 768), BF),
            vm((4, 192, 768), BF),
            vm((2, 16, 48, W), F32),
            vm((2, 16, 48, W), BF),
            vm((2, 16, 48, W), BF),
            vm((2, 4, 4, 192, 128), F32),
            vm((2, 2, 2, 192, 128), F32),
            vm((2, 2, 4, 192, 128), F32),
            vm((2, 4, 192, 128), F32),
            vm((2, 3, 192, 128), F32),
            vm((2, 4, 48, 128), F32),
            vm((2, 2, 4, 48, 128), F32),
            vm((4, 2, 48, W), F32),
            vm((W, 384), F32),
            vm((256, 384), F32),
            vm((W, 384), BF),
            vm((W, 384), BF),
            vm((256, 384), BF),
            vm((256, 384), BF),
            vm((2, 4, 128, 128), F32),
            vm((2, 3, 128, 128), F32),
            vm((2, 8, 16, 128), F32),
            vm((2, 7, 16, 128), F32),
            vm((2, 2, 4, 4, 8, 16, 128), F32),
            vm((W, W), F32),
            vm((4, W, W), BF),
            vm((W, W), F32),
            vm((W, W), F32),
            vm((48, W), F32),
            vm((48, W), F32),
            vm((W, W), F32),
            vm((W, W), F32),
            vm((W, W), F32),
            pltpu.SemaphoreType.DMA((N_MAIL,)),
            pltpu.SemaphoreType.DMA((N_MAIL,)),
            pltpu.SemaphoreType.DMA((N_LOCAL,)),
        ],
        name="selected_inverse",
        compiler_params=pltpu.CompilerParams(
            collective_id=0, has_side_effects=True, vmem_limit_bytes=VMEM_LIMIT
        ),
        cost_estimate=pl.CostEstimate(flops=4_000_000_000, bytes_accessed=8_000_000, transcendentals=0),
    )(tiles, factor_one, pattern_one, factor_two, pattern_two, coupling, diagonal_one, diagonal_two)
    free = pl.BlockSpec(memory_space=pl.ANY)
    return pl.pallas_call(
        place_kernel,
        out_shape=shapes,
        in_specs=[free] * 5,
        out_specs=(free,) * 5,
        scratch_shapes=[vm(shape.shape, F32) for shape in shapes] + [pltpu.SemaphoreType.DMA((10,))],
        name="place_results",
    )(*results)


def solution(mesh):
    return jax.shard_map(
        body,
        mesh=mesh,
        in_specs=(
            P("row", "col"),
            P(("row", "col"), None),
            P(("row", "col")),
            P(("row", "col"), None),
            P(("row", "col")),
            P(),
            P(),
            P(),
        ),
        out_specs=(P(("row", "col"), None), P(), P(("row", "col"), None), P(), P()),
        check_vma=False,
    )
```

```python
import jax
import jax.numpy as jnp
from jax import lax
from jax.experimental import pallas as pl
from jax.experimental.pallas import tpu as pltpu
from jax.sharding import PartitionSpec as P

W = 512
MESH = pl.DeviceIdType.MESH
BF = jnp.bfloat16
F32 = jnp.float32


def halves(value):
    high = value.astype(BF)
    return high, (value - high.astype(F32)).astype(BF)


def dot3(left, right):
    (lh, ll), (rh, rl) = left, right
    total = jnp.dot(lh, rh, preferred_element_type=F32)
    total += jnp.dot(lh, rl, preferred_element_type=F32)
    return total + jnp.dot(ll, rh, preferred_element_type=F32)


class Mail:
    def __init__(self, send, recv):
        self.send, self.recv, self.count, self.sent = send, recv, 0, []

    def slots(self, n):
        first = self.count
        self.count += n
        return list(range(first, first + n))

    def desc(self, slot, src, dst, dev):
        return pltpu.make_async_remote_copy(
            src, dst, self.send.at[slot], self.recv.at[slot], device_id=dev, device_id_type=MESH
        )

    def post(self, slot, src, dst, dev):
        copy = self.desc(slot, src, dst, dev)
        copy.start()
        self.sent.append(copy)

    def take(self, slot, dst, dev):
        self.desc(slot, dst, dst, dev).wait_recv()


N_MAIL = 200
N_LOCAL = 40
VMEM_LIMIT = 60 << 20


def kernel(
    res, fac1, pat1, fac2, pat2, coup, diag1, diag2,
    inv1_o, blk1_o, inv2_o, cpl_o, blk2_o,
    pat, own, rx, rh, rl, g, gh, gl, p, ra, rb, s, sb, ib, tx, fy, ft, ftb, fth, ftl, fbh, fbl,
    cb, cx, ct, cz, cf, kk_v, kb, d1_v, d2_v, o1, o2, ob1, ob2, oc,
    send, recv, local,
):
    z = lax.axis_index("row")
    col = lax.axis_index("col")
    k = col % 2
    x = (col // 2) % 4
    y = col // 8
    other = 1 - k

    def at(xx, yy, zz, kk):
        return (zz, (yy * 4 + xx) * 2 + kk)

    partner = at(x, y, z, other)

    def zdev(d):
        return at(x, y, (z + d + 8) % 8, k)

    def xdev(d):
        return at((x + d + 4) % 4, y, z, k)

    def ydev(d):
        return at(x, (y + d + 4) % 4, z, k)

    u = x + k * (y - x)
    v = y + k * (x - y)

    def udev(d):
        return at((x + (1 - k) * d + 4) % 4, (y + k * d + 4) % 4, z, k)

    def vdev(d):
        return at((x + k * d + 4) % 4, (y + (1 - k) * d + 4) % 4, z, k)

    goal = 2 * z + y // 2
    mine = (y % 2) * 4 + x
    target = at(goal % 4, goal // 4, (mine + 3 * z + 1) % 8, k)
    q = 4 * y + x
    z0 = q // 2
    chunks = {d: (z + d + 63 - 3 * z0) % 8 for d in range(-3, 5)}

    def chunk(d):
        return chunks[(d + 3) % 8 - 3]

    source = at(chunk(0) % 4, 2 * (q % 2) + chunk(0) // 4, z0, k)

    mail = Mail(send, recv)
    used = [0]

    def here(src, dst):
        copy = pltpu.make_async_copy(src, dst, local.at[used[0]])
        used[0] += 1
        copy.start()
        return copy

    load_p = [here(pat1, pat.at[0]), here(pat2, pat.at[1])]
    load_f = [here(fac1, own.at[0]), here(fac2, own.at[1])]
    load_r = [here(res.at[:, a, k], rx.at[k, a]) for a in range(4)]
    load_k = here(coup, kk_v)
    load_d1 = here(diag1, d1_v)
    load_d2 = here(diag2, d2_v)

    barrier = pltpu.get_barrier_semaphore()
    friends = [partner] + [zdev(d) for d in range(1, 8)] + [xdev(d) for d in range(1, 4)] + [ydev(d) for d in range(1, 4)]
    for dev in friends + [source]:
        pl.semaphore_signal(barrier, inc=1, device_id=dev, device_id_type=MESH)

    for j in range(2):
        load_p[j].wait()
        load_f[j].wait()
        for b in range(3):
            own[j, 16 * b : 16 * b + 16] = own[j, 16 * b : 16 * b + 16] * pat[j, b].astype(F32)
    pl.semaphore_wait(barrier, len(friends) + 1)

    slot_perm = mail.slots(2)
    slot_r = mail.slots(4)
    slot_fx = mail.slots(1)[0]

    def rows_to_column(j):
        mail.post(slot_perm[j], own.at[j], g.at[j, 2 * mine + k], target)

    def tiles_to_partner():
        for a in range(4):
            mail.post(slot_r[a], res.at[:, a, other], rx.at[k, a], partner)

    def tiles_take():
        for a in range(4):
            mail.take(slot_r[a], rx.at[other, a], partner)

    def rows_to_partner():
        fy[y, k] = own[k]
        mail.post(slot_fx, own.at[other], fy.at[y, k], partner)

    slot_up = [mail.slots(4), mail.slots(4)]
    slot_dn = [mail.slots(4), mail.slots(4)]
    slot_fwd = [mail.slots(8), mail.slots(8)]

    def split(j, m):
        gh[j, m], gl[j, m] = halves(g[j, m])

    def forward(j, f, d):
        m = 2 * chunk(d) + k
        mail.post(slot_fwd[j][f], g.at[j, m], g.at[j, m], partner)

    def split_own(j, step):
        for d in {0: (0,), 4: (4,)}.get(step, (-step, step)):
            split(j, 2 * chunk(d) + k)

    def arrived(j, f, d):
        m = 2 * chunk(d) + other
        mail.take(slot_fwd[j][f], g.at[j, m], partner)
        split(j, m)

    def ring(j, step):
        m_up = 2 * chunk(-step) + k
        m_dn = 2 * chunk(step) + k
        if step == 0:
            mail.take(slot_perm[j], g.at[j, m_up], target)
            mail.post(slot_up[j][0], g.at[j, m_up], g.at[j, m_up], zdev(1))
            mail.post(slot_dn[j][0], g.at[j, m_up], g.at[j, m_up], zdev(-1))
            return
        lo = g.at[j, m_up]
        hi = g.at[j, m_dn]
        if step == 4:
            mail.take(slot_up[j][3], lo.at[pl.ds(0, 24)], zdev(1))
            mail.take(slot_dn[j][3], hi.at[pl.ds(24, 24)], zdev(-1))
            return
        mail.take(slot_up[j][step - 1], g.at[j, m_up], zdev(1))
        if step == 3:
            mail.post(slot_up[j][3], lo.at[pl.ds(0, 24)], lo.at[pl.ds(0, 24)], zdev(1))
        else:
            mail.post(slot_up[j][step], lo, lo, zdev(1))
        mail.take(slot_dn[j][step - 1], g.at[j, m_dn], zdev(-1))
        if step == 3:
            mail.post(slot_dn[j][3], hi.at[pl.ds(24, 24)], hi.at[pl.ds(24, 24)], zdev(-1))
        else:
            mail.post(slot_dn[j][step], hi, hi, zdev(-1))

    def pass_on(j, step):
        if step in (0, 4):
            forward(j, 0 if step == 0 else 7, step)
        else:
            forward(j, 2 * step - 1, -step)
            forward(j, 2 * step, step)

    def collect(j, step):
        if step in (0, 4):
            arrived(j, 0 if step == 0 else 7, step)
        else:
            arrived(j, 2 * step - 1, -step)
            arrived(j, 2 * step, step)

    def split_r(dyn):
        for a in range(4):
            hi, lo = halves(rx[dyn, a].reshape(192, 384))
            rh[a, :, pl.ds(pl.multiple_of(dyn * 384, 128), 384)] = hi
            rl[a, :, pl.ds(pl.multiple_of(dyn * 384, 128), 384)] = lo

    def product(j):
        tiles = (rh[...].reshape(768, 768), rl[...].reshape(768, 768))
        got = dot3(tiles, (gh[j].reshape(768, W), gl[j].reshape(768, W)))
        for a in range(4):
            for b in range(4):
                p[j, a + k * (b - a), b + k * (a - b)] = got[192 * a : 192 * a + 192, 128 * b : 128 * b + 128]

    slot_a = [mail.slots(2), mail.slots(2)]
    slot_b = [mail.slots(4), mail.slots(4)]
    slot_d = [mail.slots(3), mail.slots(3)]

    def rs1_start(j):
        am, ap, an = (u + 2) % 4, (u + 1) % 4, (u + 3) % 4
        lo, hi = pl.ds(0, 2), pl.ds(2, 2)
        mail.post(slot_a[j][0], p.at[j, am, lo], ra.at[j, 0], udev(1))
        mail.post(slot_a[j][1], p.at[j, am, hi], ra.at[j, 1], udev(-1))
        mail.post(slot_b[j][0], p.at[j, ap, hi], rb.at[j, 0, hi], udev(1))
        mail.post(slot_b[j][1], p.at[j, an, lo], rb.at[j, 1, lo], udev(-1))

    def rs1_mid(j):
        ap, an = (u + 1) % 4, (u + 3) % 4
        lo, hi = pl.ds(0, 2), pl.ds(2, 2)
        mail.take(slot_a[j][0], ra.at[j, 0], udev(1))
        ra[j, 0] += p[j, ap, 0:2]
        mail.post(slot_b[j][2], ra.at[j, 0], rb.at[j, 0, lo], udev(1))
        mail.take(slot_a[j][1], ra.at[j, 1], udev(-1))
        ra[j, 1] += p[j, an, 2:4]
        mail.post(slot_b[j][3], ra.at[j, 1], rb.at[j, 1, hi], udev(-1))

    def rs1_end(j):
        lo, hi = pl.ds(0, 2), pl.ds(2, 2)
        mail.take(slot_b[j][0], rb.at[j, 0, hi], udev(1))
        mail.take(slot_b[j][1], rb.at[j, 1, lo], udev(-1))
        mail.take(slot_b[j][2], rb.at[j, 0, lo], udev(1))
        mail.take(slot_b[j][3], rb.at[j, 1, hi], udev(-1))
        for d in (2, 1, 3, 0):
            b = (v + d) % 4
            s[j, b] = p[j, u, b] + rb[j, 0, b] + rb[j, 1, b]
            if d:
                mail.post(slot_d[j][d - 1], s.at[j, b], sb.at[j, d - 1], vdev(d))

    slot_i = [mail.slots(3), mail.slots(3)]
    slot_t = mail.slots(2)

    def rs2_end(j):
        for d in range(1, 4):
            mail.take(slot_d[j][d - 1], sb.at[j, d - 1], vdev(d))
        got = s[j, v] + sb[j, 0] + sb[j, 1] + sb[j, 2]
        tx[j, k] = got.reshape(4, 48, 128)
        mail.post(slot_t[j], tx.at[j, k], tx.at[j, k], partner)

    def rows_send(j):
        ib[j, y] = tx[j, k, y]
        for d in range(1, 4):
            mail.post(slot_i[j][d - 1], tx.at[j, k, (y + d) % 4], ib.at[j, y], ydev(d))

    def rows_take(j):
        for d in range(1, 4):
            mail.take(slot_i[j][d - 1], ib.at[j, (y + 4 - d) % 4], ydev(d))
        return jnp.concatenate([ib[j, b] for b in range(4)], axis=1)

    slot_fy = mail.slots(3)
    slot_ftx = mail.slots(1)[0]

    def mates_send():
        mail.take(slot_fx, fy.at[y, other], partner)
        for d in range(1, 4):
            mail.post(slot_fy[d - 1], fy.at[y], fy.at[y], ydev(d))

    def mates_take():
        for d in range(1, 4):
            mail.take(slot_fy[d - 1], fy.at[(y + 4 - d) % 4], ydev(d))
        for c in range(2):
            ft[:, 192 * c : 192 * c + 192] = jnp.concatenate([fy[b, c] for b in range(4)], axis=0).T
        fth[...], ftl[...] = halves(ft[...])

    def mates_half():
        copy = mail.desc(slot_ftx, ft.at[pl.ds(0, 256)], ftb, partner)
        pl.when(k == 1)(copy.start)

    def mates_half_take():
        copy = mail.desc(slot_ftx, ft.at[pl.ds(0, 256)], ftb, partner)
        pl.when(k == 0)(copy.wait_recv)
        pl.when(k == 1)(copy.wait_send)

        @pl.when(k == 1)
        def _():
            ftb[...] = ft[256:512]

        fbh[...], fbl[...] = halves(ftb[...])

    slot_x = [mail.slots(3), mail.slots(3)]
    slot_z = [mail.slots(7), mail.slots(7)]
    slot_gz = [mail.slots(7), mail.slots(7)]
    slot_gu = [mail.slots(3), mail.slots(3)]
    slot_gv = [mail.slots(3), mail.slots(3)]
    slot_gc = [mail.slots(4), mail.slots(4)]
    size = (128, 64)

    def cross(j):
        mail.take(slot_t[j], tx.at[j, other], partner)
        tt = halves(jnp.concatenate([tx[j, 0].reshape(192, 128), tx[j, 1].reshape(192, 128)], axis=0))
        left = (fth[...], ftl[...]) if j == 0 else (fbh[...], fbl[...])
        got = dot3(left, tt)
        n = size[j]
        for b in range(4):
            cb[j, b, 0:n] = got[n * b : n * b + n]
        for d in (2, 1, 3):
            mail.post(slot_x[j][d - 1], cb.at[j, (x + d) % 4, pl.ds(0, n)], cx.at[j, d - 1, pl.ds(0, n)], xdev(d))

    def cross_x(j):
        n, e = size[j], size[j] // 8
        total = cb[j, x, 0:n]
        for d in range(1, 4):
            mail.take(slot_x[j][d - 1], cx.at[j, d - 1, pl.ds(0, n)], xdev(d))
            total += cx[j, d - 1, 0:n]
        for b in range(8):
            ct[j, b, 0:e] = total[e * b : e * b + e]
        for d in (4, 3, 5, 2, 6, 1, 7):
            mail.post(slot_z[j][d - 1], ct.at[j, (z + d) % 8, pl.ds(0, e)], cz.at[j, d - 1, pl.ds(0, e)], zdev(d))

    def cross_z(j):
        e = size[j] // 8
        total = ct[j, z, 0:e]
        for d in range(1, 8):
            mail.take(slot_z[j][d - 1], cz.at[j, d - 1, pl.ds(0, e)], zdev(d))
            total += cz[j, d - 1, 0:e]
        piece = cf.at[j, k, v, u, z, pl.ds(0, e)]
        piece[...] = total
        for d in (4, 3, 5, 2, 6, 1, 7):
            mail.post(slot_gz[j][d - 1], piece, piece, zdev(d))

    def cross_u(j):
        e = size[j] // 8
        for d in range(1, 8):
            mail.take(slot_gz[j][d - 1], cf.at[j, k, v, u, (z + 8 - d) % 8, pl.ds(0, e)], zdev(d))
        piece = cf.at[j, k, v, u, :, pl.ds(0, e)]
        for d in (2, 1, 3):
            mail.post(slot_gu[j][d - 1], piece, piece, udev(d))

    def cross_v(j):
        e = size[j] // 8
        for d in range(1, 4):
            mail.take(slot_gu[j][d - 1], cf.at[j, k, v, (u + 4 - d) % 4, :, pl.ds(0, e)], udev(d))
        piece = cf.at[j, k, v, :, :, pl.ds(0, e)]
        for d in (2, 1, 3):
            mail.post(slot_gv[j][d - 1], piece, piece, vdev(d))
        mail.post(slot_gc[j][0], piece, piece, partner)

    def cross_c(j):
        e = size[j] // 8
        for d in (1, 3, 2):
            piece = cf.at[j, k, (v + 4 - d) % 4, :, :, pl.ds(0, e)]
            mail.take(slot_gv[j][d - 1], piece, vdev(d))
            mail.post(slot_gc[j][d], piece, piece, partner)

    def cross_end(j):
        e = size[j] // 8
        for d in range(4):
            mail.take(slot_gc[j][d], cf.at[j, other, (u + 4 - d) % 4, :, :, pl.ds(0, e)], partner)

    def whole(c):
        parts = []
        for b in range(4):
            if c == 0:
                parts.append(cf[0, 0, b].reshape(W, 128))
            else:
                parts.append(cf[0, 1, :, b].reshape(W, 128))
        return jnp.concatenate(parts, axis=1)

    rows_to_column(0)
    tiles_to_partner()
    rows_to_partner()
    for c in load_r:
        c.wait()
    split_r(k)
    rows_to_column(1)
    ring(0, 0)
    pass_on(0, 0)
    ring(1, 0)
    pass_on(1, 0)
    mates_send()
    split_own(0, 0)
    split_own(1, 0)
    tiles_take()
    split_r(other)
    for step in (1, 2, 3):
        ring(0, step)
        ring(1, step)
        pass_on(0, step)
        pass_on(1, step)
        split_own(0, step)
        split_own(1, step)
        collect(0, step - 1)
        collect(1, step - 1)
    ring(0, 4)
    pass_on(0, 4)
    split_own(0, 4)
    collect(0, 3)
    collect(0, 4)
    product(0)
    rs1_start(0)
    ring(1, 4)
    pass_on(1, 4)
    split_own(1, 4)
    collect(1, 3)
    collect(1, 4)
    product(1)
    rs1_mid(0)
    rs1_start(1)
    mates_take()
    mates_half()
    load_k.wait()
    kb[0], kb[1] = halves(kk_v[...])
    rs1_end(0)
    rs1_mid(1)
    kb[2], kb[3] = halves(kk_v[...].T)
    rs2_end(0)
    mates_half_take()
    cross(0)
    rows_send(0)
    rs1_end(1)
    cross_x(0)
    rs2_end(1)
    cross(1)
    rows_send(1)
    cross_z(0)
    cross_x(1)
    cross_u(0)
    cross_z(1)
    cross_v(0)
    cross_u(1)
    cross_v(1)
    t_own = rows_take(0)
    o1[...] = -t_own
    out1 = here(o1, inv1_o)
    o2[...] = dot3(halves(t_own), (kb[0], kb[1])) - rows_take(1)
    out2 = here(o2, inv2_o)
    cross_c(0)
    cross_end(0)
    load_d1.wait()
    load_d2.wait()
    ob1[...] = d1_v[...] + whole(0)
    out3 = here(ob1, blk1_o)
    c21 = whole(1)
    oc[...] = c21.T - dot3(halves(ob1[...]), (kb[0], kb[1]))
    out4 = here(oc, cpl_o)
    cross_c(1)
    ob2[...] = d2_v[...] - dot3(halves(c21), (kb[0], kb[1])) - dot3((kb[2], kb[3]), halves(oc[...]))
    cross_end(1)
    for b in range(4):
        for a in range(4):
            cols = slice(128 * b, 128 * b + 128)
            ob2[64 * a : 64 * a + 64, cols] += cf[1, 0, b, a, :, 0:8].reshape(64, 128)
            ob2[256 + 64 * a : 320 + 64 * a, cols] += cf[1, 1, a, b, :, 0:8].reshape(64, 128)
    out5 = here(ob2, blk2_o)
    for copy in mail.sent:
        copy.wait_send()
    for copy in (out1, out2, out3, out4, out5):
        copy.wait()


def place_kernel(*refs):
    held, sem = refs[10:15], refs[15]
    loads = [pltpu.make_async_copy(refs[i], held[i], sem.at[i]) for i in range(5)]
    stores = [pltpu.make_async_copy(held[i], refs[5 + i], sem.at[5 + i]) for i in range(5)]
    for copy in loads:
        copy.start()
    for load, store in zip(loads, stores):
        load.wait()
        store.start()
    for copy in stores:
        copy.wait()


def body(resident, factor_one, pattern_one, factor_two, pattern_two, coupling, diagonal_one, diagonal_two):
    tiles = resident.reshape(4, 4, 2, 48, 384)
    vm = pltpu.VMEM
    any_ = pl.BlockSpec(memory_space=pltpu.HBM)
    sds = jax.ShapeDtypeStruct
    shapes = (sds((48, W), F32), sds((W, W), F32), sds((48, W), F32), sds((W, W), F32), sds((W, W), F32))
    results = pl.pallas_call(
        kernel,
        out_shape=shapes,
        in_specs=[any_] * 8,
        out_specs=(any_,) * 5,
        scratch_shapes=[
            pltpu.SMEM((2, 3), jnp.int32),
            vm((2, 48, W), F32),
            vm((2, 4, 4, 48, 384), F32),
            vm((4, 192, 768), BF),
            vm((4, 192, 768), BF),
            vm((2, 16, 48, W), F32),
            vm((2, 16, 48, W), BF),
            vm((2, 16, 48, W), BF),
            vm((2, 4, 4, 192, 128), F32),
            vm((2, 2, 2, 192, 128), F32),
            vm((2, 2, 4, 192, 128), F32),
            vm((2, 4, 192, 128), F32),
            vm((2, 3, 192, 128), F32),
            vm((2, 4, 48, 128), F32),
            vm((2, 2, 4, 48, 128), F32),
            vm((4, 2, 48, W), F32),
            vm((W, 384), F32),
            vm((256, 384), F32),
            vm((W, 384), BF),
            vm((W, 384), BF),
            vm((256, 384), BF),
            vm((256, 384), BF),
            vm((2, 4, 128, 128), F32),
            vm((2, 3, 128, 128), F32),
            vm((2, 8, 16, 128), F32),
            vm((2, 7, 16, 128), F32),
            vm((2, 2, 4, 4, 8, 16, 128), F32),
            vm((W, W), F32),
            vm((4, W, W), BF),
            vm((W, W), F32),
            vm((W, W), F32),
            vm((48, W), F32),
            vm((48, W), F32),
            vm((W, W), F32),
            vm((W, W), F32),
            vm((W, W), F32),
            pltpu.SemaphoreType.DMA((N_MAIL,)),
            pltpu.SemaphoreType.DMA((N_MAIL,)),
            pltpu.SemaphoreType.DMA((N_LOCAL,)),
        ],
        name="selected_inverse",
        compiler_params=pltpu.CompilerParams(
            collective_id=0, has_side_effects=True, vmem_limit_bytes=VMEM_LIMIT
        ),
        cost_estimate=pl.CostEstimate(flops=4_000_000_000, bytes_accessed=8_000_000, transcendentals=0),
    )(tiles, factor_one, pattern_one, factor_two, pattern_two, coupling, diagonal_one, diagonal_two)
    free = pl.BlockSpec(memory_space=pl.ANY)
    return pl.pallas_call(
        place_kernel,
        out_shape=shapes,
        in_specs=[free] * 5,
        out_specs=(free,) * 5,
        scratch_shapes=[vm(shape.shape, F32) for shape in shapes] + [pltpu.SemaphoreType.DMA((10,))],
        name="place_results",
    )(*results)


def solution(mesh):
    return jax.shard_map(
        body,
        mesh=mesh,
        in_specs=(
            P("row", "col"),
            P(("row", "col"), None),
            P(("row", "col")),
            P(("row", "col"), None),
            P(("row", "col")),
            P(),
            P(),
            P(),
        ),
        out_specs=(P(("row", "col"), None), P(), P(("row", "col"), None), P(), P()),
        check_vma=False,
    )
```

```python
import jax
import jax.numpy as jnp
from jax import lax
from jax.experimental import pallas as pl
from jax.experimental.pallas import tpu as pltpu
from jax.sharding import PartitionSpec as P

W = 512
MESH = pl.DeviceIdType.MESH
BF = jnp.bfloat16
F32 = jnp.float32


def halves(value):
    high = value.astype(BF)
    return high, (value - high.astype(F32)).astype(BF)


def dot3(left, right):
    (lh, ll), (rh, rl) = left, right
    total = jnp.dot(lh, rh, preferred_element_type=F32)
    total += jnp.dot(lh, rl, preferred_element_type=F32)
    return total + jnp.dot(ll, rh, preferred_element_type=F32)


class Mail:
    def __init__(self, send, recv):
        self.send, self.recv, self.count, self.sent = send, recv, 0, []

    def slots(self, n):
        first = self.count
        self.count += n
        return list(range(first, first + n))

    def desc(self, slot, src, dst, dev):
        return pltpu.make_async_remote_copy(
            src, dst, self.send.at[slot], self.recv.at[slot], device_id=dev, device_id_type=MESH
        )

    def post(self, slot, src, dst, dev):
        copy = self.desc(slot, src, dst, dev)
        copy.start()
        self.sent.append(copy)

    def take(self, slot, dst, dev):
        self.desc(slot, dst, dst, dev).wait_recv()


N_MAIL = 200
N_LOCAL = 40
VMEM_LIMIT = 60 << 20


def kernel(
    res, fac1, pat1, fac2, pat2, coup, diag1, diag2,
    inv1_o, blk1_o, inv2_o, cpl_o, blk2_o,
    pat, own, rx, rh, rl, g, gh, gl, p, ra, rb, s, sb, ib, tx, fy, ft, ftb, fth, ftl, fbh, fbl,
    cb, cx, ct, cz, cf, kk_v, kb, d1_v, d2_v, o1, o2, ob1, ob2, oc,
    send, recv, local,
):
    z = lax.axis_index("row")
    col = lax.axis_index("col")
    k = col % 2
    x = (col // 2) % 4
    y = col // 8
    other = 1 - k

    def at(xx, yy, zz, kk):
        return (zz, (yy * 4 + xx) * 2 + kk)

    partner = at(x, y, z, other)

    def zdev(d):
        return at(x, y, (z + d + 8) % 8, k)

    def xdev(d):
        return at((x + d + 4) % 4, y, z, k)

    def ydev(d):
        return at(x, (y + d + 4) % 4, z, k)

    u = x + k * (y - x)
    v = y + k * (x - y)

    def udev(d):
        return at((x + (1 - k) * d + 4) % 4, (y + k * d + 4) % 4, z, k)

    def vdev(d):
        return at((x + k * d + 4) % 4, (y + (1 - k) * d + 4) % 4, z, k)

    goal = 2 * z + y // 2
    mine = (y % 2) * 4 + x
    target = at(goal % 4, goal // 4, (mine + 3 * z + 1) % 8, k)
    q = 4 * y + x
    z0 = q // 2
    chunks = {d: (z + d + 63 - 3 * z0) % 8 for d in range(-3, 5)}

    def chunk(d):
        return chunks[(d + 3) % 8 - 3]

    source = at(chunk(0) % 4, 2 * (q % 2) + chunk(0) // 4, z0, k)

    mail = Mail(send, recv)
    used = [0]

    def here(src, dst):
        copy = pltpu.make_async_copy(src, dst, local.at[used[0]])
        used[0] += 1
        copy.start()
        return copy

    load_p = [here(pat1, pat.at[0]), here(pat2, pat.at[1])]
    load_f = [here(fac1, own.at[0]), here(fac2, own.at[1])]
    load_r = [here(res.at[:, a, k], rx.at[k, a]) for a in range(4)]
    load_k = here(coup, kk_v)
    load_d1 = here(diag1, d1_v)
    load_d2 = here(diag2, d2_v)

    barrier = pltpu.get_barrier_semaphore()
    friends = [partner] + [zdev(d) for d in range(1, 8)] + [xdev(d) for d in range(1, 4)] + [ydev(d) for d in range(1, 4)]
    for dev in friends + [source]:
        pl.semaphore_signal(barrier, inc=1, device_id=dev, device_id_type=MESH)

    for j in range(2):
        load_p[j].wait()
        load_f[j].wait()
        for b in range(3):
            own[j, 16 * b : 16 * b + 16] = own[j, 16 * b : 16 * b + 16] * pat[j, b].astype(F32)
    pl.semaphore_wait(barrier, len(friends) + 1)

    slot_perm = mail.slots(2)
    slot_r = mail.slots(4)
    slot_fx = mail.slots(1)[0]

    def rows_to_column(j):
        mail.post(slot_perm[j], own.at[j], g.at[j, 2 * mine + k], target)

    def tiles_to_partner():
        for a in range(4):
            mail.post(slot_r[a], res.at[:, a, other], rx.at[k, a], partner)

    def tiles_take():
        for a in range(4):
            mail.take(slot_r[a], rx.at[other, a], partner)

    def rows_to_partner():
        fy[y, k] = own[k]
        mail.post(slot_fx, own.at[other], fy.at[y, k], partner)

    slot_up = [mail.slots(4), mail.slots(4)]
    slot_dn = [mail.slots(4), mail.slots(4)]
    slot_fwd = [mail.slots(8), mail.slots(8)]

    def split(j, m):
        gh[j, m], gl[j, m] = halves(g[j, m])

    def forward(j, f, d):
        m = 2 * chunk(d) + k
        mail.post(slot_fwd[j][f], g.at[j, m], g.at[j, m], partner)

    def split_own(j, step):
        for d in {0: (0,), 4: (4,)}.get(step, (-step, step)):
            split(j, 2 * chunk(d) + k)

    def arrived(j, f, d):
        m = 2 * chunk(d) + other
        mail.take(slot_fwd[j][f], g.at[j, m], partner)
        split(j, m)

    def ring(j, step):
        m_up = 2 * chunk(-step) + k
        m_dn = 2 * chunk(step) + k
        if step == 0:
            mail.take(slot_perm[j], g.at[j, m_up], target)
            mail.post(slot_up[j][0], g.at[j, m_up], g.at[j, m_up], zdev(1))
            mail.post(slot_dn[j][0], g.at[j, m_up], g.at[j, m_up], zdev(-1))
            return
        lo = g.at[j, m_up]
        hi = g.at[j, m_dn]
        if step == 4:
            mail.take(slot_up[j][3], lo.at[pl.ds(0, 24)], zdev(1))
            mail.take(slot_dn[j][3], hi.at[pl.ds(24, 24)], zdev(-1))
            return
        mail.take(slot_up[j][step - 1], g.at[j, m_up], zdev(1))
        if step == 3:
            mail.post(slot_up[j][3], lo.at[pl.ds(0, 24)], lo.at[pl.ds(0, 24)], zdev(1))
        else:
            mail.post(slot_up[j][step], lo, lo, zdev(1))
        mail.take(slot_dn[j][step - 1], g.at[j, m_dn], zdev(-1))
        if step == 3:
            mail.post(slot_dn[j][3], hi.at[pl.ds(24, 24)], hi.at[pl.ds(24, 24)], zdev(-1))
        else:
            mail.post(slot_dn[j][step], hi, hi, zdev(-1))

    def pass_on(j, step):
        if step in (0, 4):
            forward(j, 0 if step == 0 else 7, step)
        else:
            forward(j, 2 * step - 1, -step)
            forward(j, 2 * step, step)

    def collect(j, step):
        if step in (0, 4):
            arrived(j, 0 if step == 0 else 7, step)
        else:
            arrived(j, 2 * step - 1, -step)
            arrived(j, 2 * step, step)

    def split_r(dyn):
        for a in range(4):
            hi, lo = halves(rx[dyn, a].reshape(192, 384))
            rh[a, :, pl.ds(pl.multiple_of(dyn * 384, 128), 384)] = hi
            rl[a, :, pl.ds(pl.multiple_of(dyn * 384, 128), 384)] = lo

    def product(j):
        tiles = (rh[...].reshape(768, 768), rl[...].reshape(768, 768))
        got = dot3(tiles, (gh[j].reshape(768, W), gl[j].reshape(768, W)))
        for a in range(4):
            for b in range(4):
                p[j, a + k * (b - a), b + k * (a - b)] = got[192 * a : 192 * a + 192, 128 * b : 128 * b + 128]

    slot_a = [mail.slots(2), mail.slots(2)]
    slot_b = [mail.slots(4), mail.slots(4)]
    slot_d = [mail.slots(3), mail.slots(3)]

    def rs1_start(j):
        am, ap, an = (u + 2) % 4, (u + 1) % 4, (u + 3) % 4
        lo, hi = pl.ds(0, 2), pl.ds(2, 2)
        mail.post(slot_a[j][0], p.at[j, am, lo], ra.at[j, 0], udev(1))
        mail.post(slot_a[j][1], p.at[j, am, hi], ra.at[j, 1], udev(-1))
        mail.post(slot_b[j][0], p.at[j, ap, hi], rb.at[j, 0, hi], udev(1))
        mail.post(slot_b[j][1], p.at[j, an, lo], rb.at[j, 1, lo], udev(-1))

    def rs1_mid(j):
        ap, an = (u + 1) % 4, (u + 3) % 4
        lo, hi = pl.ds(0, 2), pl.ds(2, 2)
        mail.take(slot_a[j][0], ra.at[j, 0], udev(1))
        ra[j, 0] += p[j, ap, 0:2]
        mail.post(slot_b[j][2], ra.at[j, 0], rb.at[j, 0, lo], udev(1))
        mail.take(slot_a[j][1], ra.at[j, 1], udev(-1))
        ra[j, 1] += p[j, an, 2:4]
        mail.post(slot_b[j][3], ra.at[j, 1], rb.at[j, 1, hi], udev(-1))

    def rs1_end(j):
        lo, hi = pl.ds(0, 2), pl.ds(2, 2)
        mail.take(slot_b[j][0], rb.at[j, 0, hi], udev(1))
        mail.take(slot_b[j][1], rb.at[j, 1, lo], udev(-1))
        mail.take(slot_b[j][2], rb.at[j, 0, lo], udev(1))
        mail.take(slot_b[j][3], rb.at[j, 1, hi], udev(-1))
        for d in (2, 1, 3, 0):
            b = (v + d) % 4
            s[j, b] = p[j, u, b] + rb[j, 0, b] + rb[j, 1, b]
            if d:
                mail.post(slot_d[j][d - 1], s.at[j, b], sb.at[j, d - 1], vdev(d))

    slot_i = [mail.slots(3), mail.slots(3)]
    slot_t = mail.slots(2)

    def rs2_end(j):
        for d in range(1, 4):
            mail.take(slot_d[j][d - 1], sb.at[j, d - 1], vdev(d))
        got = s[j, v] + sb[j, 0] + sb[j, 1] + sb[j, 2]
        tx[j, k] = got.reshape(4, 48, 128)
        mail.post(slot_t[j], tx.at[j, k], tx.at[j, k], partner)

    def rows_send(j):
        ib[j, y] = tx[j, k, y]
        for d in range(1, 4):
            mail.post(slot_i[j][d - 1], tx.at[j, k, (y + d) % 4], ib.at[j, y], ydev(d))

    def rows_take(j):
        for d in range(1, 4):
            mail.take(slot_i[j][d - 1], ib.at[j, (y + 4 - d) % 4], ydev(d))
        return jnp.concatenate([ib[j, b] for b in range(4)], axis=1)

    slot_fy = mail.slots(3)
    slot_ftx = mail.slots(1)[0]

    def mates_send():
        mail.take(slot_fx, fy.at[y, other], partner)
        for d in range(1, 4):
            mail.post(slot_fy[d - 1], fy.at[y], fy.at[y], ydev(d))

    def mates_take():
        for d in range(1, 4):
            mail.take(slot_fy[d - 1], fy.at[(y + 4 - d) % 4], ydev(d))
        for c in range(2):
            ft[:, 192 * c : 192 * c + 192] = jnp.concatenate([fy[b, c] for b in range(4)], axis=0).T
        fth[...], ftl[...] = halves(ft[...])

    def mates_half():
        copy = mail.desc(slot_ftx, ft.at[pl.ds(0, 256)], ftb, partner)
        pl.when(k == 1)(copy.start)

    def mates_half_take():
        copy = mail.desc(slot_ftx, ft.at[pl.ds(0, 256)], ftb, partner)
        pl.when(k == 0)(copy.wait_recv)
        pl.when(k == 1)(copy.wait_send)

        @pl.when(k == 1)
        def _():
            ftb[...] = ft[256:512]

        fbh[...], fbl[...] = halves(ftb[...])

    slot_x = [mail.slots(3), mail.slots(3)]
    slot_z = [mail.slots(7), mail.slots(7)]
    slot_gz = [mail.slots(7), mail.slots(7)]
    slot_gu = [mail.slots(3), mail.slots(3)]
    slot_gv = [mail.slots(3), mail.slots(3)]
    slot_gc = [mail.slots(4), mail.slots(4)]
    size = (128, 64)

    def cross(j):
        mail.take(slot_t[j], tx.at[j, other], partner)
        tt = halves(jnp.concatenate([tx[j, 0].reshape(192, 128), tx[j, 1].reshape(192, 128)], axis=0))
        left = (fth[...], ftl[...]) if j == 0 else (fbh[...], fbl[...])
        got = dot3(left, tt)
        n = size[j]
        for b in range(4):
            cb[j, b, 0:n] = got[n * b : n * b + n]
        for d in (2, 1, 3):
            mail.post(slot_x[j][d - 1], cb.at[j, (x + d) % 4, pl.ds(0, n)], cx.at[j, d - 1, pl.ds(0, n)], xdev(d))

    def cross_x(j):
        n, e = size[j], size[j] // 8
        total = cb[j, x, 0:n]
        for d in range(1, 4):
            mail.take(slot_x[j][d - 1], cx.at[j, d - 1, pl.ds(0, n)], xdev(d))
            total += cx[j, d - 1, 0:n]
        for b in range(8):
            ct[j, b, 0:e] = total[e * b : e * b + e]
        for d in (4, 3, 5, 2, 6, 1, 7):
            mail.post(slot_z[j][d - 1], ct.at[j, (z + d) % 8, pl.ds(0, e)], cz.at[j, d - 1, pl.ds(0, e)], zdev(d))

    def cross_z(j):
        e = size[j] // 8
        total = ct[j, z, 0:e]
        for d in range(1, 8):
            mail.take(slot_z[j][d - 1], cz.at[j, d - 1, pl.ds(0, e)], zdev(d))
            total += cz[j, d - 1, 0:e]
        piece = cf.at[j, k, v, u, z, pl.ds(0, e)]
        piece[...] = total
        for d in (4, 3, 5, 2, 6, 1, 7):
            mail.post(slot_gz[j][d - 1], piece, piece, zdev(d))

    def cross_u(j):
        e = size[j] // 8
        for d in range(1, 8):
            mail.take(slot_gz[j][d - 1], cf.at[j, k, v, u, (z + 8 - d) % 8, pl.ds(0, e)], zdev(d))
        piece = cf.at[j, k, v, u, :, pl.ds(0, e)]
        for d in (2, 1, 3):
            mail.post(slot_gu[j][d - 1], piece, piece, udev(d))

    def cross_v(j):
        e = size[j] // 8
        for d in range(1, 4):
            mail.take(slot_gu[j][d - 1], cf.at[j, k, v, (u + 4 - d) % 4, :, pl.ds(0, e)], udev(d))
        piece = cf.at[j, k, v, :, :, pl.ds(0, e)]
        for d in (2, 1, 3):
            mail.post(slot_gv[j][d - 1], piece, piece, vdev(d))
        mail.post(slot_gc[j][0], piece, piece, partner)

    def cross_c(j):
        e = size[j] // 8
        for d in (1, 3, 2):
            piece = cf.at[j, k, (v + 4 - d) % 4, :, :, pl.ds(0, e)]
            mail.take(slot_gv[j][d - 1], piece, vdev(d))
            mail.post(slot_gc[j][d], piece, piece, partner)

    def cross_end(j):
        e = size[j] // 8
        for d in range(4):
            mail.take(slot_gc[j][d], cf.at[j, other, (u + 4 - d) % 4, :, :, pl.ds(0, e)], partner)

    def whole(c):
        parts = []
        for b in range(4):
            if c == 0:
                parts.append(cf[0, 0, b].reshape(W, 128))
            else:
                parts.append(cf[0, 1, :, b].reshape(W, 128))
        return jnp.concatenate(parts, axis=1)

    rows_to_column(0)
    tiles_to_partner()
    rows_to_partner()
    for c in load_r:
        c.wait()
    split_r(k)
    rows_to_column(1)
    ring(0, 0)
    pass_on(0, 0)
    ring(1, 0)
    pass_on(1, 0)
    mates_send()
    split_own(0, 0)
    split_own(1, 0)
    tiles_take()
    split_r(other)
    for step in (1, 2, 3):
        ring(0, step)
        ring(1, step)
        pass_on(0, step)
        pass_on(1, step)
        split_own(0, step)
        split_own(1, step)
        collect(0, step - 1)
        collect(1, step - 1)
    ring(0, 4)
    pass_on(0, 4)
    split_own(0, 4)
    collect(0, 3)
    collect(0, 4)
    product(0)
    rs1_start(0)
    ring(1, 4)
    pass_on(1, 4)
    split_own(1, 4)
    collect(1, 3)
    collect(1, 4)
    product(1)
    rs1_mid(0)
    rs1_start(1)
    mates_take()
    mates_half()
    load_k.wait()
    kb[0], kb[1] = halves(kk_v[...])
    rs1_end(0)
    rs1_mid(1)
    kb[2], kb[3] = halves(kk_v[...].T)
    rs2_end(0)
    mates_half_take()
    cross(0)
    rows_send(0)
    rs1_end(1)
    cross_x(0)
    rs2_end(1)
    cross(1)
    rows_send(1)
    cross_z(0)
    cross_x(1)
    t_own = rows_take(0)
    o1[...] = -t_own
    out1 = here(o1, inv1_o)
    cross_u(0)
    cross_z(1)
    o2[...] = dot3(halves(t_own), (kb[0], kb[1])) - rows_take(1)
    out2 = here(o2, inv2_o)
    cross_v(0)
    cross_u(1)
    cross_v(1)
    cross_c(0)
    cross_end(0)
    load_d1.wait()
    load_d2.wait()
    ob1[...] = d1_v[...] + whole(0)
    out3 = here(ob1, blk1_o)
    cross_c(1)
    c21 = whole(1)
    oc[...] = c21.T - dot3(halves(ob1[...]), (kb[0], kb[1]))
    out4 = here(oc, cpl_o)
    oh = halves(oc[...])
    cross_end(1)
    out5 = []
    for c in range(2):
        rows = slice(256 * c, 256 * c + 256)
        got = d2_v[rows] - dot3(halves(c21[rows]), (kb[0], kb[1])) - dot3((kb[2, rows], kb[3, rows]), oh)
        if c == 0:
            last = [cf[1, 0, b, :, :, 0:8].reshape(256, 128) for b in range(4)]
        else:
            last = [cf[1, 1, :, b, :, 0:8].reshape(256, 128) for b in range(4)]
        ob2[rows] = got + jnp.concatenate(last, axis=1)
        out5.append(here(ob2.at[pl.ds(256 * c, 256)], blk2_o.at[pl.ds(256 * c, 256)]))
    for copy in mail.sent:
        copy.wait_send()
    for copy in (out1, out2, out3, out4, *out5):
        copy.wait()


def place_kernel(*refs):
    held, sem = refs[10:15], refs[15]
    parts = [(0, 0, 48), (2, 0, 48)] + [(i, n, 256) for i in (1, 3, 4) for n in (0, 256)]
    loads, stores = [], []
    for at, (i, first, n) in enumerate(parts):
        rows = pl.ds(first, n)
        loads.append(pltpu.make_async_copy(refs[i].at[rows], held[i].at[rows], sem.at[at]))
        stores.append(pltpu.make_async_copy(held[i].at[rows], refs[5 + i].at[rows], sem.at[8 + at]))
        loads[at].start()
    for load, store in zip(loads, stores):
        load.wait()
        store.start()
    for copy in stores:
        copy.wait()


def body(resident, factor_one, pattern_one, factor_two, pattern_two, coupling, diagonal_one, diagonal_two):
    tiles = resident.reshape(4, 4, 2, 48, 384)
    vm = pltpu.VMEM
    any_ = pl.BlockSpec(memory_space=pltpu.HBM)
    sds = jax.ShapeDtypeStruct
    shapes = (sds((48, W), F32), sds((W, W), F32), sds((48, W), F32), sds((W, W), F32), sds((W, W), F32))
    results = pl.pallas_call(
        kernel,
        out_shape=shapes,
        in_specs=[any_] * 8,
        out_specs=(any_,) * 5,
        scratch_shapes=[
            pltpu.SMEM((2, 3), jnp.int32),
            vm((2, 48, W), F32),
            vm((2, 4, 4, 48, 384), F32),
            vm((4, 192, 768), BF),
            vm((4, 192, 768), BF),
            vm((2, 16, 48, W), F32),
            vm((2, 16, 48, W), BF),
            vm((2, 16, 48, W), BF),
            vm((2, 4, 4, 192, 128), F32),
            vm((2, 2, 2, 192, 128), F32),
            vm((2, 2, 4, 192, 128), F32),
            vm((2, 4, 192, 128), F32),
            vm((2, 3, 192, 128), F32),
            vm((2, 4, 48, 128), F32),
            vm((2, 2, 4, 48, 128), F32),
            vm((4, 2, 48, W), F32),
            vm((W, 384), F32),
            vm((256, 384), F32),
            vm((W, 384), BF),
            vm((W, 384), BF),
            vm((256, 384), BF),
            vm((256, 384), BF),
            vm((2, 4, 128, 128), F32),
            vm((2, 3, 128, 128), F32),
            vm((2, 8, 16, 128), F32),
            vm((2, 7, 16, 128), F32),
            vm((2, 2, 4, 4, 8, 16, 128), F32),
            vm((W, W), F32),
            vm((4, W, W), BF),
            vm((W, W), F32),
            vm((W, W), F32),
            vm((48, W), F32),
            vm((48, W), F32),
            vm((W, W), F32),
            vm((W, W), F32),
            vm((W, W), F32),
            pltpu.SemaphoreType.DMA((N_MAIL,)),
            pltpu.SemaphoreType.DMA((N_MAIL,)),
            pltpu.SemaphoreType.DMA((N_LOCAL,)),
        ],
        name="selected_inverse",
        compiler_params=pltpu.CompilerParams(
            collective_id=0, has_side_effects=True, vmem_limit_bytes=VMEM_LIMIT
        ),
        cost_estimate=pl.CostEstimate(flops=4_000_000_000, bytes_accessed=8_000_000, transcendentals=0),
    )(tiles, factor_one, pattern_one, factor_two, pattern_two, coupling, diagonal_one, diagonal_two)
    free = pl.BlockSpec(memory_space=pl.ANY)
    return pl.pallas_call(
        place_kernel,
        out_shape=shapes,
        in_specs=[free] * 5,
        out_specs=(free,) * 5,
        scratch_shapes=[vm(shape.shape, F32) for shape in shapes] + [pltpu.SemaphoreType.DMA((16,))],
        name="place_results",
    )(*results)


def solution(mesh):
    return jax.shard_map(
        body,
        mesh=mesh,
        in_specs=(
            P("row", "col"),
            P(("row", "col"), None),
            P(("row", "col")),
            P(("row", "col"), None),
            P(("row", "col")),
            P(),
            P(),
            P(),
        ),
        out_specs=(P(("row", "col"), None), P(), P(("row", "col"), None), P(), P()),
        check_vma=False,
    )
```
